32 devices in a mesh: seq: 8 (over z, x), head: 4 (over y, core).
Axes of the slice: x: 2, y: 2, z: 4, core: 2. Of those that a mesh axis runs over, the one named last changes fastest.
Arguments:
- qkv_pre: bfloat16 [4096, 3, 16, 128], P(('seq', 'head')), may hold values from -10 to 10
- grad_out: bfloat16 [4096, 2048], P(('seq', 'head')), may hold values from -48 to 48
- out_values: bfloat16 [2048, 2048], P('head'), may hold values from -4 to 4
- out_scales: float32 [16, 16], replicated, may hold values from 0.01 to 0.04
- conv_kernel: float32 [31, 3, 16, 128], P(None, None, 'head'), may hold values from -1 to 1
- window: int32 [16], replicated, may hold values from 64 to 96, as said below
- offsets: int32 [8], replicated, may hold values from 0 to 32, as said below
Outputs:
- grad_pre: bfloat16 [4096, 3, 16, 128], P(('seq', 'head'))
The draws below stay inside these ranges and needn't reach their ends.
Inputs may be any that keep to these rules, and one draw needn't show every extreme that they name: window[h] + offsets[b] <= 128 for every head h and block b; some head has window exactly 96. offsets[b] <= 32 for every block b, with equality in at least one block.
All inputs are finite; a program needn't handle non-finite values.
Results may differ from the reference program's by a relative error of at most 0.005.
The reference program's roundings to bfloat16 on the way count: a program that leaves them out, or rounds other values in their place, can miss the bound.
Values may be sent and summed in bfloat16 or wider, within the bound.
No kernel may reach another device: no remote copies, remote signals or barrier semaphores. Data moves between devices by JAX's collectives and lax.ppermute only.
A program may use at most 64 MiB of HBM per device.

```python
import math
import jax
import jax.numpy as jnp
from jax import lax

HEADS = 16
HEAD_DIM = 128
KW = 31
SCALE_BLOCK = 128
MASKB = 512
WIDTH = 2048
ROWS = 512
TOKENS = 4096
SPAN = 128
NBLOCKS = 8


def draw_conv_kernel(key, part):
    first_tap = jax.random.uniform(jax.random.fold_in(key, 1), (1, 3, HEADS, HEAD_DIM), jnp.float32, 0.5, 1.0)
    later_taps = 0.15 * jax.random.truncated_normal(jax.random.fold_in(key, 2), -4.0, 4.0, (KW - 1, 3, HEADS, HEAD_DIM), jnp.float32)
    return jnp.concatenate([first_tap, later_taps], axis=0)


def window_and_offsets(key):
    base_key = jax.random.fold_in(key, 101)
    top_window = SPAN - SPAN // 4
    window = jax.random.randint(jax.random.fold_in(base_key, 1), (HEADS,), SPAN // 2, top_window + 1, jnp.int32)
    widest = jax.random.randint(jax.random.fold_in(base_key, 4), (), 0, HEADS, jnp.int32)
    window = jnp.where(jnp.arange(HEADS, dtype=jnp.int32) == widest, top_window, window)
    top_offset = SPAN // 4
    raw_draw = jax.random.randint(jax.random.fold_in(base_key, 2), (NBLOCKS,), 0, 1 << 20, jnp.int32)
    offsets = raw_draw % (top_offset + 1)
    chosen = jax.random.randint(jax.random.fold_in(base_key, 3), (), 0, NBLOCKS, jnp.int32)
    offsets = jnp.where(jnp.arange(NBLOCKS, dtype=jnp.int32) == chosen, top_offset, offsets)
    return (window, offsets)


def draw_window(key, part):
    return window_and_offsets(key)[0]


def draw_offsets(key, part):
    return window_and_offsets(key)[1]


def draw_qkv_pre(key, part):
    shape = (TOKENS, 3, HEADS, HEAD_DIM)
    return jax.random.truncated_normal(key, -6.0, 6.0, shape, jnp.float32).astype(jnp.bfloat16)


def block_scale(stream_key, extent, pieces, smallest, largest):
    loudness = 1.0
    for position, parts in pieces:
        heights = jax.random.uniform(jax.random.fold_in(jax.random.fold_in(stream_key, 6), position), (parts,), jnp.float32, smallest / len(pieces), largest / len(pieces))
        loudness = loudness * jnp.repeat(jnp.exp(heights), extent[position] // parts).reshape((-1,) + (1,) * (len(extent) - 1 - position))
    return loudness


def bell_draw(key, dims, scale, reach, split=(), kind=jnp.bfloat16):
    factor_of = block_scale(key, dims, split, -0.22, 0.18) if split else 1.0
    values = jax.random.normal(key, dims, jnp.float32) * scale * factor_of
    return jnp.minimum(jnp.maximum(values, -reach), reach).astype(kind)


def setup_inputs(seed: int = 0) -> dict:
    key_list = jax.random.split(jax.random.key(seed), 8)
    return {
        "qkv_pre": draw_qkv_pre(jax.random.fold_in(key_list[7], 71), 0),
        "grad_out": bell_draw(key_list[1], (TOKENS, WIDTH), 8.0, 48.0, ((0, 32),)),
        "out_values": bell_draw(key_list[2], (WIDTH, WIDTH), 1.0, 4.0, ((0, 4),)),
        "out_scales": jnp.clip(jnp.exp(jax.random.uniform(key_list[3], (WIDTH // SCALE_BLOCK, WIDTH // SCALE_BLOCK), jnp.float32, math.log(0.01), math.log(0.04))), 0.01, 0.04),
        "conv_kernel": draw_conv_kernel(jax.random.fold_in(key_list[7], 71), 0),
        "window": draw_window(jax.random.fold_in(key_list[7], 71), 0),
        "offsets": draw_offsets(jax.random.fold_in(key_list[7], 71), 0),
    }


def causal_conv(series, kernel):
    length = series.shape[0]
    padded = jnp.concatenate([jnp.zeros((KW - 1,) + series.shape[1:], series.dtype), series], axis=0)
    summed = jnp.zeros(series.shape, jnp.float32)
    for kernel_tap in range(KW):
        first_row = KW - 1 - kernel_tap
        summed = summed + kernel[kernel_tap] * padded[first_row:first_row + length].astype(jnp.float32)
    return summed

def transposed_parts(g_own, g_cross, kernel):
    length = g_own.shape[0]
    tail_zeros = jnp.zeros((KW - 1,) + g_own.shape[1:], jnp.float32)
    own_pad = jnp.concatenate([g_own, tail_zeros], axis=0)
    cross_pad = jnp.concatenate([g_cross, tail_zeros], axis=0)
    block_of = jnp.arange(length + KW - 1, dtype=jnp.int32) // ROWS
    home = block_of[:length]
    own_sum = jnp.zeros(g_own.shape, jnp.float32)
    carry_sum = jnp.zeros(g_own.shape, jnp.float32)
    for kernel_tap in range(KW):
        target = block_of[kernel_tap:kernel_tap + length]
        same_block = (target == home)[:, None, None]
        next_block = (target == home + 1)[:, None, None]
        shifted_own = own_pad[kernel_tap:kernel_tap + length]
        shifted_cross = cross_pad[kernel_tap:kernel_tap + length]
        own_sum = own_sum + kernel[kernel_tap] * jnp.where(same_block, shifted_own, 0.0)
        carry_sum = carry_sum + kernel[kernel_tap] * (jnp.where(same_block, shifted_cross, 0.0) + jnp.where(next_block, shifted_own, 0.0))
    carry_b = lax.optimization_barrier(carry_sum.astype(jnp.bfloat16))
    return (own_sum + carry_b.astype(jnp.float32)).astype(jnp.bfloat16)

def reference(qkv_pre, grad_out, out_values, out_scales, conv_kernel, window, offsets):
    expanded = jnp.repeat(jnp.repeat(out_scales, SCALE_BLOCK, axis=0), SCALE_BLOCK, axis=1)
    weight = (out_values.astype(jnp.float32) * expanded).astype(jnp.bfloat16)
    inv_scale = 1.0 / math.sqrt(HEAD_DIM)
    key_len = SPAN + MASKB

    def per_head(head):
        reach_all = lax.dynamic_index_in_dim(window, head, 0, keepdims=False) + offsets
        head_rows = lax.dynamic_slice_in_dim(weight, head * HEAD_DIM, HEAD_DIM, 0)
        d_attn = lax.dot_general(grad_out, head_rows, (((1,), (1,)), ((), ())), preferred_element_type=jnp.float32).astype(jnp.bfloat16)
        series = lax.dynamic_index_in_dim(qkv_pre, head, 2, keepdims=False)
        kernel = lax.dynamic_index_in_dim(conv_kernel, head, 2, keepdims=False)
        mixed = causal_conv(series, kernel).astype(jnp.bfloat16)
        query_rows = mixed[:, 0]
        pad_zeros = jnp.zeros((SPAN, HEAD_DIM), jnp.bfloat16)
        key_pad = jnp.concatenate([pad_zeros, mixed[:, 1]], axis=0)
        value_pad = jnp.concatenate([pad_zeros, mixed[:, 2]], axis=0)

        def attend(totals, block_index):
            k_own, k_cross, v_own, v_cross = totals
            q_start = block_index * MASKB
            q_block = lax.dynamic_slice_in_dim(query_rows, q_start, MASKB, 0)
            o_block = lax.dynamic_slice_in_dim(d_attn, q_start, MASKB, 0)
            k_block = lax.dynamic_slice_in_dim(key_pad, q_start, key_len, 0)
            v_block = lax.dynamic_slice_in_dim(value_pad, q_start, key_len, 0)
            scores = jnp.dot(q_block, k_block.T, preferred_element_type=jnp.float32) * inv_scale
            query_pos = q_start + jnp.arange(MASKB, dtype=jnp.int32)
            key_pos = q_start - SPAN + jnp.arange(key_len, dtype=jnp.int32)
            distance = query_pos[:, None] - key_pos[None, :]
            reach_now = reach_all[block_index]
            allowed = (distance >= 0) & (distance <= reach_now) & (key_pos[None, :] >= 0)
            row_top = lax.optimization_barrier(jnp.max(jnp.where(allowed, scores, -1e+30), axis=1, keepdims=True))
            exp_scores = jnp.where(allowed, jnp.exp(scores - row_top), 0.0)
            probs = exp_scores / lax.optimization_barrier(jnp.sum(exp_scores, axis=1, keepdims=True))
            probs_b = probs.astype(jnp.bfloat16)
            d_prob = jnp.dot(o_block, v_block.T, preferred_element_type=jnp.float32)
            row_delta = lax.optimization_barrier(jnp.sum(probs * d_prob, axis=1, keepdims=True))
            d_score = (probs * (d_prob - row_delta) * inv_scale).astype(jnp.bfloat16)
            grad_q_block = jnp.dot(d_score, k_block, preferred_element_type=jnp.float32)
            grad_k_block = jnp.dot(d_score.T, q_block, preferred_element_type=jnp.float32)
            grad_v_block = jnp.dot(probs_b.T, o_block, preferred_element_type=jnp.float32)
            same_block = (key_pos >= q_start // ROWS * ROWS)[:, None]

            def add_into(buffer, addend):
                current = lax.dynamic_slice_in_dim(buffer, q_start, key_len, 0)
                return lax.dynamic_update_slice_in_dim(buffer, current + addend, q_start, 0)
            k_own = add_into(k_own, jnp.where(same_block, grad_k_block, 0.0))
            k_cross = add_into(k_cross, jnp.where(same_block, 0.0, grad_k_block))
            v_own = add_into(v_own, jnp.where(same_block, grad_v_block, 0.0))
            v_cross = add_into(v_cross, jnp.where(same_block, 0.0, grad_v_block))
            return ((k_own, k_cross, v_own, v_cross), grad_q_block)
        empty = jnp.zeros((SPAN + TOKENS, HEAD_DIM), jnp.float32)
        totals, grad_q_blocks = lax.scan(attend, (empty, empty, empty, empty), jnp.arange(NBLOCKS, dtype=jnp.int32))
        k_own, k_cross, v_own, v_cross = totals
        grad_q = grad_q_blocks.reshape(TOKENS, HEAD_DIM)
        g_own = jnp.stack([grad_q, k_own[SPAN:], v_own[SPAN:]], axis=1)
        g_cross = jnp.stack([jnp.zeros_like(grad_q), k_cross[SPAN:], v_cross[SPAN:]], axis=1)
        return transposed_parts(g_own, g_cross, kernel)
    per_heads = lax.map(per_head, jnp.arange(HEADS, dtype=jnp.int32))
    return jnp.transpose(per_heads, (1, 2, 0, 3))
```

```python
import functools
import math

import jax
import jax.numpy as jnp
from jax import lax
from jax.experimental import pallas as pl
from jax.experimental.pallas import tpu as pltpu
from jax.sharding import PartitionSpec as P

KW = 31
MASKB = 512
TILE = 128
PAD = 32
NEG = -1e30
F32 = jnp.float32
BF16 = jnp.bfloat16
VMEM_LIMIT = 56 * 1024 * 1024


def params():
    return pltpu.CompilerParams(vmem_limit_bytes=VMEM_LIMIT)


def loop(count, body):
    if count <= 4:
        for i in range(count):
            body(i)
    else:
        lax.fori_loop(0, count, lambda i, c: (body(i), c)[1], 0)


def pack_kernel(n_head, n_chunks, src, *refs):
    outs, stage = refs[:-1], refs[-1]
    tokens, _, heads, dim = src.shape
    local = heads // n_head
    per_chunk = local // n_chunks
    me = lax.axis_index("head")
    stage[...] = src[:, 0].astype(F32).reshape(tokens * heads, dim)
    for j in range(n_head):
        first = jnp.bitwise_xor(me, j) * local
        for c in range(n_chunks):
            for h in range(per_chunk):
                rows = stage[pl.ds(first + c * per_chunk + h, tokens, stride=heads), :]
                outs[j * n_chunks + c][0, h] = rows.astype(BF16)


def pack(qkv, n_head, n_chunks):
    tokens, parts, heads, dim = qkv.shape
    per_chunk = heads // n_head // n_chunks
    count = n_head * n_chunks
    outs = pl.pallas_call(
        functools.partial(pack_kernel, n_head, n_chunks),
        grid=(parts,),
        in_specs=[pl.BlockSpec((tokens, 1, heads, dim), lambda p: (0, p, 0, 0))],
        out_specs=[pl.BlockSpec((1, per_chunk, tokens, dim), lambda p: (p, 0, 0, 0))] * count,
        out_shape=[jax.ShapeDtypeStruct((parts, per_chunk, tokens, dim), BF16)] * count,
        scratch_shapes=[pltpu.VMEM((tokens * heads, dim), F32)],
        compiler_params=params(),
        name="pack",
    )(qkv)
    return [[outs[j * n_chunks + c] for j in range(n_head)] for c in range(n_chunks)]


def unpack_kernel(n_head, n_chunks, *refs):
    srcs, out, stage = refs[:-2], refs[-2], refs[-1]
    tokens, _, heads, dim = out.shape
    local = heads // n_head
    per_chunk = local // n_chunks
    me = lax.axis_index("head")
    for j in range(n_head):
        first = jnp.bitwise_xor(me, j) * local
        for c in range(n_chunks):
            for h in range(per_chunk):
                rows = srcs[c * n_head + j][0, h].astype(F32)
                stage[pl.ds(first + c * per_chunk + h, tokens, stride=heads), :] = rows
    out[:, 0] = stage[...].reshape(tokens, heads, dim).astype(BF16)


def unpack(pieces, n_head, n_chunks):
    parts, per_chunk, tokens, dim = pieces[0][0].shape
    heads = per_chunk * n_chunks * n_head
    flat = [piece for chunk in pieces for piece in chunk]
    return pl.pallas_call(
        functools.partial(unpack_kernel, n_head, n_chunks),
        grid=(parts,),
        in_specs=[pl.BlockSpec((1, per_chunk, tokens, dim), lambda p: (p, 0, 0, 0))] * len(flat),
        out_specs=pl.BlockSpec((tokens, 1, heads, dim), lambda p: (0, p, 0, 0)),
        out_shape=jax.ShapeDtypeStruct((tokens, parts, heads, dim), BF16),
        scratch_shapes=[pltpu.VMEM((tokens * heads, dim), F32)],
        compiler_params=params(),
        name="unpack",
    )(*flat)


def dequant_kernel(values, scales, weight):
    rows, width = values.shape
    side = width // scales.shape[1]
    first = lax.axis_index("head") * (rows // side)
    for r in range(rows // side):
        for c in range(width // side):
            at = (slice(r * side, (r + 1) * side), slice(c * side, (c + 1) * side))
            weight[at] = (values[at].astype(F32) * scales[first + r, c]).astype(BF16)


def dequantize(values, scales):
    return pl.pallas_call(
        dequant_kernel,
        in_specs=[
            pl.BlockSpec(memory_space=pltpu.VMEM),
            pl.BlockSpec(memory_space=pltpu.SMEM),
        ],
        out_specs=pl.BlockSpec(memory_space=pltpu.VMEM),
        out_shape=jax.ShapeDtypeStruct(values.shape, BF16),
        compiler_params=params(),
        name="dequant",
    )(values, scales)


def dattn_kernel(grads, weight, out):
    heads, _, dim = out.shape
    full = lax.dot_general(
        grads[...], weight[...], (((1,), (1,)), ((), ())), preferred_element_type=F32
    )
    for h in range(heads):
        out[h] = full[:, h * dim : (h + 1) * dim].astype(BF16)


def d_attn(grads, weight, dim):
    tokens = grads.shape[0]
    heads = weight.shape[0] // dim
    return pl.pallas_call(
        dattn_kernel,
        out_shape=jax.ShapeDtypeStruct((heads, tokens, dim), BF16),
        compiler_params=params(),
        name="dattn",
    )(grads, weight)


def core_kernel(n_head, head0, span, window, offsets, *refs):
    pieces = refs[:n_head]
    grads = refs[n_head : 2 * n_head]
    halo, taps, own_out, carry_out, ext, mixed, d_out, totals = refs[2 * n_head :]
    tokens = pieces[0].shape[2]
    seq_rows = tokens * n_head
    margin = span + PAD
    keys = span + TILE
    dim = pieces[0].shape[3]
    inv_scale = 1.0 / math.sqrt(dim)
    me = lax.axis_index("head")
    seq_index = lax.axis_index("seq")
    head = head0 + pl.program_id(0)
    local = taps.shape[2]

    ext[1, :margin] = halo[0, :margin].astype(F32)
    ext[2, :margin] = halo[0, margin : 2 * margin].astype(F32)
    ext[0, span:margin] = halo[0, 2 * margin :].astype(F32)
    for j in range(n_head):
        start = pl.multiple_of(jnp.bitwise_xor(me, j) * tokens, tokens)
        for p in range(3):
            ext[p, pl.ds(margin + start, tokens), :] = pieces[j][p, 0].astype(F32)
        d_out[pl.ds(start, tokens), :] = grads[j][0]

    def tap(p, tau):
        return taps[tau, p, pl.ds(head, 1), :]

    def conv_block(p, first, rows):
        acc = jnp.zeros((rows, dim), F32)
        for b in range(8):
            window_rows = ext[p, pl.ds(first + 8 - b, rows + 24), :]
            for a in range(4):
                tau = 8 * a + b
                if tau < KW:
                    acc = acc + tap(p, tau) * window_rows[24 - 8 * a : 24 - 8 * a + rows]
        mixed[p, pl.ds(first, rows), :] = acc.astype(BF16)

    def conv_part(p):
        lax.fori_loop(
            0,
            (span + seq_rows) // TILE,
            lambda i, c: (conv_block(p, pl.multiple_of(i * TILE, TILE), TILE), c)[1],
            0,
        )

    lax.fori_loop(1, 3, lambda p, c: (conv_part(p), c)[1], 0)
    lax.fori_loop(
        0,
        seq_rows // TILE,
        lambda i, c: (conv_block(0, pl.multiple_of(span + i * TILE, TILE), TILE), c)[1],
        0,
    )

    totals[1] = jnp.zeros(totals.shape[1:], F32)
    totals[2] = jnp.zeros(totals.shape[1:], F32)
    totals[0, span:margin] = jnp.zeros((PAD, dim), F32)
    totals[0, margin + seq_rows :] = jnp.zeros((PAD, dim), F32)
    row = lax.broadcasted_iota(jnp.int32, (TILE, keys), 0)
    col = lax.broadcasted_iota(jnp.int32, (TILE, keys), 1)
    distance = row + span - col
    base = window[me * local + head]
    blocks = seq_rows // MASKB

    def attend(t):
        first = t * TILE
        reach = base + offsets[seq_index * blocks + first // MASKB]
        limit = jnp.minimum(reach, seq_index * seq_rows + first + row)
        allowed = (distance >= 0) & (distance <= limit)
        q = mixed[0, pl.ds(span + first, TILE), :]
        k = mixed[1, pl.ds(first, keys), :]
        v = mixed[2, pl.ds(first, keys), :]
        o = d_out[pl.ds(first, TILE), :]
        nt = (((1,), (1,)), ((), ()))
        tn = (((0,), (0,)), ((), ()))
        scores = lax.dot_general(q, k, nt, preferred_element_type=F32) * inv_scale
        scores = jnp.where(allowed, scores, NEG)
        top = jnp.max(scores, axis=1, keepdims=True)
        exps = jnp.where(allowed, jnp.exp(scores - top), 0.0)
        probs = exps / jnp.sum(exps, axis=1, keepdims=True)
        d_prob = lax.dot_general(o, v, nt, preferred_element_type=F32)
        delta = jnp.sum(probs * d_prob, axis=1, keepdims=True)
        d_score = (probs * (d_prob - delta) * inv_scale).astype(BF16)
        probs_b = probs.astype(BF16)
        totals[0, pl.ds(margin + first, TILE), :] = jnp.dot(d_score, k, preferred_element_type=F32)
        at = pl.ds(PAD + first, keys)
        totals[1, at, :] += lax.dot_general(d_score, q, tn, preferred_element_type=F32)
        totals[2, at, :] += lax.dot_general(probs_b, o, tn, preferred_element_type=F32)

    loop(seq_rows // TILE, attend)

    def spread_block(p, first, rows):
        acc = jnp.zeros((rows, dim), F32)
        for b in range(8):
            window_rows = totals[p, pl.ds(first + b, rows + 24), :]
            for a in range(4):
                tau = 8 * a + b
                if tau < KW:
                    acc = acc + tap(p, tau) * window_rows[8 * a : 8 * a + rows]
        return acc

    def own_block(p, i):
        first = pl.multiple_of(i * TILE, TILE)
        own_out[p, 0, pl.ds(first, TILE), :] = spread_block(p, margin + first, TILE)

    carry_out[0, 2 * margin :] = spread_block(0, span, PAD).astype(BF16)
    for p in (1, 2):
        for first in range(0, margin, PAD):
            at = (p - 1) * margin + first
            carry_out[0, at : at + PAD] = spread_block(p, first, PAD).astype(BF16)
    lax.fori_loop(
        0,
        3,
        lambda p, c: lax.fori_loop(
            0, seq_rows // TILE, lambda i, d: (own_block(p, i), d)[1], c
        ),
        0,
    )


def core(pieces, grads, halo, taps, window, offsets, head0, span):
    n_head = len(pieces)
    parts, heads, tokens, dim = pieces[0].shape
    seq_rows = tokens * n_head
    margin = span + PAD
    return pl.pallas_call(
        functools.partial(core_kernel, n_head, head0, span),
        grid=(heads,),
        in_specs=[pl.BlockSpec(memory_space=pltpu.SMEM)] * 2
        + [pl.BlockSpec((parts, 1, tokens, dim), lambda h: (0, h, 0, 0))] * n_head
        + [pl.BlockSpec((1, tokens, dim), lambda h: (head0 + h, 0, 0))] * n_head
        + [
            pl.BlockSpec((1, 2 * margin + PAD, dim), lambda h: (h, 0, 0)),
            pl.BlockSpec(taps.shape, lambda h: (0, 0, 0, 0)),
        ],
        out_specs=[
            pl.BlockSpec((parts, 1, seq_rows, dim), lambda h: (0, h, 0, 0)),
            pl.BlockSpec((1, 2 * margin + PAD, dim), lambda h: (h, 0, 0)),
        ],
        out_shape=[
            jax.ShapeDtypeStruct((parts, heads, seq_rows, dim), F32),
            jax.ShapeDtypeStruct((heads, 2 * margin + PAD, dim), BF16),
        ],
        scratch_shapes=[
            pltpu.VMEM((parts, margin + seq_rows, dim), F32),
            pltpu.VMEM((parts, span + seq_rows, dim), BF16),
            pltpu.VMEM((seq_rows, dim), BF16),
            pltpu.VMEM((parts, margin + seq_rows + PAD, dim), F32),
        ],
        compiler_params=params(),
        name="core",
    )(window, offsets, *pieces, *grads, halo, taps)


def finish_kernel(n_head, span, own, carry, *refs):
    outs, whole = refs[:-1], refs[-1]
    tokens = outs[0].shape[2]
    seq_rows = own.shape[2]
    margin = span + PAD
    me = lax.axis_index("head")
    for p, size, start in ((0, PAD, 2 * margin), (1, margin, 0), (2, margin, margin)):
        edge = seq_rows - size
        whole[p, :edge] = own[p, 0, :edge].astype(BF16)
        back = carry[0, start : start + size].astype(F32)
        whole[p, edge:] = (own[p, 0, edge:] + back).astype(BF16)
    for j in range(n_head):
        start = pl.multiple_of(jnp.bitwise_xor(me, j) * tokens, tokens)
        for p in range(3):
            outs[j][p, 0] = whole[p, pl.ds(start, tokens), :]


def finish(own, carry, n_head, span):
    parts, heads, seq_rows, dim = own.shape
    tokens = seq_rows // n_head
    return pl.pallas_call(
        functools.partial(finish_kernel, n_head, span),
        grid=(heads,),
        in_specs=[
            pl.BlockSpec((parts, 1, seq_rows, dim), lambda h: (0, h, 0, 0)),
            pl.BlockSpec((1, carry.shape[1], dim), lambda h: (h, 0, 0)),
        ],
        out_specs=[pl.BlockSpec((parts, 1, tokens, dim), lambda h: (0, h, 0, 0))] * n_head,
        out_shape=[jax.ShapeDtypeStruct((parts, heads, tokens, dim), BF16)] * n_head,
        scratch_shapes=[pltpu.VMEM((parts, seq_rows, dim), BF16)],
        compiler_params=params(),
        name="finish",
    )(own, carry)


def partner(value, j):
    if j == 0:
        return value
    size = lax.axis_size("head")
    return lax.ppermute(value, "head", [(i, i ^ j) for i in range(size)])


def shifted(value, by):
    length = lax.axis_size("seq")
    pairs = [(i, i + by) for i in range(length) if 0 <= i + by < length]
    return lax.ppermute(value, "seq", pairs)


def tail_of(pieces, p, rows):
    me = lax.axis_index("head")
    n_head = len(pieces)
    tokens = pieces[0].shape[2]
    found = []
    source = n_head - 1
    while rows > 0:
        take = min(rows, tokens)
        parts = [piece[p, :, tokens - take :] for piece in pieces]
        found.insert(0, lax.select_n(jnp.bitwise_xor(me, source), *parts))
        rows -= take
        source -= 1
    return found


def per_device(qkv_pre, grad_out, out_values, out_scales, conv_kernel, window, offsets):
    n_head = lax.axis_size("head")
    tokens, _, heads, dim = qkv_pre.shape
    local = heads // n_head
    n_chunks = 2 if local % 2 == 0 else 1
    per_chunk = local // n_chunks
    seq_rows = tokens * n_head
    span = seq_rows // 4
    margin = span + PAD

    packed = pack(qkv_pre, n_head, n_chunks)
    g_pieces = [grad_out]
    for j in range(1, n_head):
        if j > 1 and j % 2 == 1:
            g_pieces.append(partner(g_pieces[j - 1], 1))
        else:
            g_pieces.append(partner(grad_out, j))
    weight = dequantize(out_values, out_scales)
    grads = [d_attn(g, weight, dim) for g in g_pieces]

    results = []
    for c in range(n_chunks):
        pieces = [partner(packed[c][j], j) for j in range(n_head)]
        tail = jnp.concatenate(
            tail_of(pieces, 1, margin) + tail_of(pieces, 2, margin) + tail_of(pieces, 0, PAD), axis=1
        )
        halo = shifted(tail, 1)
        own, carry = core(
            pieces, grads, halo, conv_kernel, window, offsets, c * per_chunk, span
        )
        outs = finish(own, shifted(carry, -1), n_head, span)
        results.append([partner(outs[j], j) for j in range(n_head)])
    return unpack(results, n_head, n_chunks)


def solution(mesh):
    return jax.shard_map(
        per_device,
        mesh=mesh,
        in_specs=(
            P(("seq", "head"), None, None, None),
            P(("seq", "head"), None),
            P("head", None),
            P(),
            P(None, None, "head", None),
            P(),
            P(),
        ),
        out_specs=P(("seq", "head"), None, None, None),
        check_vma=False,
    )
```

```python
import functools
import math

import jax
import jax.numpy as jnp
from jax import lax
from jax.experimental import pallas as pl
from jax.experimental.pallas import tpu as pltpu
from jax.sharding import PartitionSpec as P

KW = 31
MASKB = 512
TILE = 128
PAD = 32
NEG = -1e30
F32 = jnp.float32
BF16 = jnp.bfloat16
MIB = 1024 * 1024
NT = (((1,), (1,)), ((), ()))
TN = (((0,), (0,)), ((), ()))


def call(kernel, mib, **kw):
    return pl.pallas_call(
        kernel,
        compiler_params=pltpu.CompilerParams(vmem_limit_bytes=mib * MIB),
        cost_estimate=pl.CostEstimate(flops=1000, bytes_accessed=1000, transcendentals=0),
        **kw,
    )


def loop(count, body):
    if count <= 4:
        for i in range(count):
            body(i)
    else:
        lax.fori_loop(0, count, lambda i, c: (body(i), c)[1], 0)


def pack_kernel(n_head, n_chunks, src, *refs):
    outs, stage = refs[:-1], refs[-1]
    heads = src.shape[2]
    local = heads // n_head
    per_chunk = local // n_chunks
    me = lax.axis_index("head")
    stage[...] = jnp.swapaxes(src[:, 0], 0, 1)
    for j in range(n_head):
        first = jnp.bitwise_xor(me, j) * local
        for c in range(n_chunks):
            for h in range(per_chunk):
                outs[j * n_chunks + c][0, h] = stage[first + c * per_chunk + h]


def pack(qkv, n_head, n_chunks):
    tokens, parts, heads, dim = qkv.shape
    per_chunk = heads // n_head // n_chunks
    count = n_head * n_chunks
    outs = call(
        functools.partial(pack_kernel, n_head, n_chunks),
        8,
        grid=(parts,),
        in_specs=[pl.BlockSpec((tokens, 1, heads, dim), lambda p: (0, p, 0, 0))],
        out_specs=[pl.BlockSpec((1, per_chunk, tokens, dim), lambda p: (p, 0, 0, 0))] * count,
        out_shape=[jax.ShapeDtypeStruct((parts, per_chunk, tokens, dim), BF16)] * count,
        scratch_shapes=[pltpu.VMEM((heads, tokens, dim), BF16)],
        name="pack",
    )(qkv)
    return [[outs[j * n_chunks + c] for j in range(n_head)] for c in range(n_chunks)]


def unpack_kernel(n_head, n_chunks, *refs):
    srcs, out, stage = refs[:-2], refs[-2], refs[-1]
    heads = out.shape[2]
    local = heads // n_head
    per_chunk = local // n_chunks
    me = lax.axis_index("head")
    for j in range(n_head):
        first = jnp.bitwise_xor(me, j) * local
        for c in range(n_chunks):
            for h in range(per_chunk):
                stage[first + c * per_chunk + h] = srcs[c * n_head + j][0, h]
    out[:, 0] = jnp.swapaxes(stage[...], 0, 1)


def unpack(pieces, n_head, n_chunks):
    parts, per_chunk, tokens, dim = pieces[0][0].shape
    heads = per_chunk * n_chunks * n_head
    flat = [piece for chunk in pieces for piece in chunk]
    return call(
        functools.partial(unpack_kernel, n_head, n_chunks),
        8,
        grid=(parts,),
        in_specs=[pl.BlockSpec((1, per_chunk, tokens, dim), lambda p: (p, 0, 0, 0))] * len(flat),
        out_specs=pl.BlockSpec((tokens, 1, heads, dim), lambda p: (0, p, 0, 0)),
        out_shape=jax.ShapeDtypeStruct((tokens, parts, heads, dim), BF16),
        scratch_shapes=[pltpu.VMEM((heads, tokens, dim), BF16)],
        name="unpack",
    )(*flat)


def dequant_kernel(side, values, scales, weight):
    rows, width = values.shape
    first = lax.axis_index("head") * (rows // side)
    for r in range(rows // side):
        for c in range(width // side):
            block = values[r * side : (r + 1) * side, c * side : (c + 1) * side].astype(F32)
            block = block * scales[first + r, pl.program_id(0) * (width // side) + c]
            weight[c * side : (c + 1) * side, r * side : (r + 1) * side] = block.T.astype(BF16)


def dequantize(values, scales):
    rows, width = values.shape
    side = width // scales.shape[1]
    step = 4 * side
    return call(
        functools.partial(dequant_kernel, side),
        8,
        grid=(width // step,),
        in_specs=[
            pl.BlockSpec((rows, step), lambda i: (0, i)),
            pl.BlockSpec(memory_space=pltpu.SMEM),
        ],
        out_specs=pl.BlockSpec((step, rows), lambda i: (i, 0)),
        out_shape=jax.ShapeDtypeStruct((width, rows), BF16),
        name="dequant",
    )(values, scales)


def dattn_kernel(count, *refs):
    weight = refs[count]
    for grads, out in zip(refs[:count], refs[count + 1 :]):
        out[...] = jnp.dot(grads[...], weight[...], preferred_element_type=F32).astype(BF16)


def d_attn(pieces, weight):
    out = jax.ShapeDtypeStruct((pieces[0].shape[0], weight.shape[1]), BF16)
    return call(
        functools.partial(dattn_kernel, len(pieces)),
        12,
        out_shape=[out] * len(pieces),
        name="dattn",
    )(*pieces, weight)


def spread(totals, taps, head, p, first, rows):
    acc = jnp.zeros((rows, totals.shape[-1]), F32)
    for b in range(8):
        window_rows = totals[p, pl.ds(first + b, rows + 24), :]
        for a in range(4):
            tau = 8 * a + b
            if tau < KW:
                acc = acc + taps[tau, p, pl.ds(head, 1), :] * window_rows[8 * a : 8 * a + rows]
    return acc


def core_kernel(n_head, head0, span, window, offsets, *refs):
    pieces = refs[:n_head]
    grads = refs[n_head : 2 * n_head]
    halo, taps, totals_out, carry_out, ext, mixed, d_out = refs[2 * n_head :]
    totals = totals_out.at[:, 0]
    tokens = pieces[0].shape[2]
    seq_rows = tokens * n_head
    margin = span + PAD
    keys = span + TILE
    dim = pieces[0].shape[3]
    inv_scale = 1.0 / math.sqrt(dim)
    me = lax.axis_index("head")
    seq_index = lax.axis_index("seq")
    head = head0 + pl.program_id(0)
    local = taps.shape[2]

    ext[1, :margin] = halo[0, :margin].astype(F32)
    ext[2, :margin] = halo[0, margin : 2 * margin].astype(F32)
    ext[0, span:margin] = halo[0, 2 * margin :].astype(F32)
    for j in range(n_head):
        start = pl.multiple_of(jnp.bitwise_xor(me, j) * tokens, tokens)
        for p in range(3):
            ext[p, pl.ds(margin + start, tokens), :] = pieces[j][p, 0].astype(F32)
        d_out[pl.ds(start, tokens), :] = grads[j][...]

    def tap(p, tau):
        return taps[tau, p, pl.ds(head, 1), :]

    def conv_block(p, first, rows):
        acc = jnp.zeros((rows, dim), F32)
        for b in range(8):
            window_rows = ext[p, pl.ds(first + 8 - b, rows + 24), :]
            for a in range(4):
                tau = 8 * a + b
                if tau < KW:
                    acc = acc + tap(p, tau) * window_rows[24 - 8 * a : 24 - 8 * a + rows]
        mixed[p, pl.ds(first, rows), :] = acc.astype(BF16)

    def conv_part(p):
        lax.fori_loop(
            0,
            (span + seq_rows) // TILE,
            lambda i, c: (conv_block(p, pl.multiple_of(i * TILE, TILE), TILE), c)[1],
            0,
        )

    lax.fori_loop(1, 3, lambda p, c: (conv_part(p), c)[1], 0)
    lax.fori_loop(
        0,
        seq_rows // TILE,
        lambda i, c: (conv_block(0, pl.multiple_of(span + i * TILE, TILE), TILE), c)[1],
        0,
    )

    totals[1] = jnp.zeros(totals.shape[1:], F32)
    totals[2] = jnp.zeros(totals.shape[1:], F32)
    totals[0, span:margin] = jnp.zeros((PAD, dim), F32)
    totals[0, margin + seq_rows :] = jnp.zeros((PAD, dim), F32)
    row = lax.broadcasted_iota(jnp.int32, (TILE, keys), 0)
    col = lax.broadcasted_iota(jnp.int32, (TILE, keys), 1)
    distance = row + span - col
    base = window[me * local + head]
    blocks = seq_rows // MASKB

    def attend(t):
        first = t * TILE
        reach = base + offsets[seq_index * blocks + first // MASKB]
        limit = jnp.minimum(reach, seq_index * seq_rows + first + row)
        allowed = (distance >= 0) & (distance <= limit)
        q = mixed[0, pl.ds(span + first, TILE), :]
        k = mixed[1, pl.ds(first, keys), :]
        v = mixed[2, pl.ds(first, keys), :]
        o = d_out[pl.ds(first, TILE), :]
        scores = lax.dot_general(q, k, NT, preferred_element_type=F32) * inv_scale
        scores = jnp.where(allowed, scores, NEG)
        top = jnp.max(scores, axis=1, keepdims=True)
        exps = jnp.where(allowed, jnp.exp(scores - top), 0.0)
        probs = exps / jnp.sum(exps, axis=1, keepdims=True)
        d_prob = lax.dot_general(o, v, NT, preferred_element_type=F32)
        delta = jnp.sum(probs * d_prob, axis=1, keepdims=True)
        d_score = (probs * (d_prob - delta) * inv_scale).astype(BF16)
        probs_b = probs.astype(BF16)
        totals[0, pl.ds(margin + first, TILE), :] = jnp.dot(d_score, k, preferred_element_type=F32)
        at = pl.ds(PAD + first, keys)
        totals[1, at, :] += lax.dot_general(d_score, q, TN, preferred_element_type=F32)
        totals[2, at, :] += lax.dot_general(probs_b, o, TN, preferred_element_type=F32)

    loop(seq_rows // TILE, attend)

    carry_out[0, 2 * margin :] = spread(totals, taps, head, 0, span, PAD).astype(BF16)
    for p in (1, 2):
        for first in range(0, margin, PAD):
            at = (p - 1) * margin + first
            carry_out[0, at : at + PAD] = spread(totals, taps, head, p, first, PAD).astype(BF16)


def core(pieces, grads, halo, taps, window, offsets, head0, span):
    n_head = len(pieces)
    parts, heads, tokens, dim = pieces[0].shape
    seq_rows = tokens * n_head
    margin = span + PAD
    return call(
        functools.partial(core_kernel, n_head, head0, span),
        16,
        grid=(heads,),
        in_specs=[pl.BlockSpec(memory_space=pltpu.SMEM)] * 2
        + [pl.BlockSpec((parts, 1, tokens, dim), lambda h: (0, h, 0, 0))] * n_head
        + [pl.BlockSpec((tokens, dim), lambda h: (0, head0 + h))] * n_head
        + [
            pl.BlockSpec((1, 2 * margin + PAD, dim), lambda h: (h, 0, 0)),
            pl.BlockSpec(taps.shape, lambda h: (0, 0, 0, 0)),
        ],
        out_specs=[
            pl.BlockSpec((parts, 1, margin + seq_rows + PAD, dim), lambda h: (0, h, 0, 0)),
            pl.BlockSpec((1, 2 * margin + PAD, dim), lambda h: (h, 0, 0)),
        ],
        out_shape=[
            jax.ShapeDtypeStruct((parts, heads, margin + seq_rows + PAD, dim), F32),
            jax.ShapeDtypeStruct((heads, 2 * margin + PAD, dim), BF16),
        ],
        scratch_shapes=[
            pltpu.VMEM((parts, margin + seq_rows, dim), F32),
            pltpu.VMEM((parts, span + seq_rows, dim), BF16),
            pltpu.VMEM((seq_rows, dim), BF16),
        ],
        name="core",
    )(window, offsets, *pieces, *grads, halo, taps)


def finish_kernel(n_head, head0, span, totals, carry, taps, *refs):
    outs, edge = refs[:-1], refs[-1]
    tokens = outs[0].shape[2]
    seq_rows = tokens * n_head
    margin = span + PAD
    me = lax.axis_index("head")
    head = head0 + pl.program_id(0)
    rows = totals.at[:, 0]

    @pl.when(pl.program_id(0) == 0)
    def _():
        edge[...] = jnp.zeros(edge.shape, F32)

    for p, size, start in ((0, PAD, 2 * margin), (1, margin, 0), (2, margin, margin)):
        edge[p, seq_rows - size :] = carry[0, start : start + size].astype(F32)
    for j in range(n_head):
        start = pl.multiple_of(jnp.bitwise_xor(me, j) * tokens, tokens)

        def part(p, c, j=j, start=start):
            own = spread(rows, taps, head, p, margin + start, tokens)
            outs[j][p, 0] = (own + edge[p, pl.ds(start, tokens), :]).astype(BF16)
            return c

        lax.fori_loop(0, 3, part, 0)


def finish(totals, carry, taps, head0, n_head, span):
    parts, heads, rows, dim = totals.shape
    seq_rows = rows - span - 2 * PAD
    tokens = seq_rows // n_head
    return call(
        functools.partial(finish_kernel, n_head, head0, span),
        16,
        grid=(heads,),
        in_specs=[
            pl.BlockSpec((parts, 1, rows, dim), lambda h: (0, h, 0, 0)),
            pl.BlockSpec((1, carry.shape[1], dim), lambda h: (h, 0, 0)),
            pl.BlockSpec(taps.shape, lambda h: (0, 0, 0, 0)),
        ],
        out_specs=[pl.BlockSpec((parts, 1, tokens, dim), lambda h: (0, h, 0, 0))] * n_head,
        out_shape=[jax.ShapeDtypeStruct((parts, heads, tokens, dim), BF16)] * n_head,
        scratch_shapes=[pltpu.VMEM((parts, seq_rows, dim), F32)],
        name="finish",
    )(totals, carry, taps)


def partner(value, j):
    if j == 0:
        return value
    size = lax.axis_size("head")
    return lax.ppermute(value, "head", [(i, i ^ j) for i in range(size)])


def shifted(value, by):
    length = lax.axis_size("seq")
    pairs = [(i, i + by) for i in range(length) if 0 <= i + by < length]
    return lax.ppermute(value, "seq", pairs)


def tail_of(pieces, p, rows):
    me = lax.axis_index("head")
    n_head = len(pieces)
    tokens = pieces[0].shape[2]
    found = []
    source = n_head - 1
    while rows > 0:
        take = min(rows, tokens)
        parts = [piece[p, :, tokens - take :] for piece in pieces]
        found.insert(0, lax.select_n(jnp.bitwise_xor(me, source), *parts))
        rows -= take
        source -= 1
    return found


def per_device(qkv_pre, grad_out, out_values, out_scales, conv_kernel, window, offsets):
    n_head = lax.axis_size("head")
    tokens, _, heads, dim = qkv_pre.shape
    local = heads // n_head
    n_chunks = 2 if local % 2 == 0 else 1
    per_chunk = local // n_chunks
    seq_rows = tokens * n_head
    span = seq_rows // 4
    margin = span + PAD

    packed = pack(qkv_pre, n_head, n_chunks)
    g_pieces = [grad_out]
    for j in range(1, n_head):
        if j > 1 and j % 2 == 1:
            g_pieces.append(partner(g_pieces[j - 1], 1))
        else:
            g_pieces.append(partner(grad_out, j))
    weight = dequantize(out_values, out_scales)
    grads = []
    for j in range(0, n_head, 2):
        grads += d_attn(g_pieces[j : j + 2], weight)

    carried = []
    for c in range(n_chunks):
        pieces = [partner(packed[c][j], j) for j in range(n_head)]
        tail = jnp.concatenate(
            tail_of(pieces, 1, margin) + tail_of(pieces, 2, margin) + tail_of(pieces, 0, PAD), axis=1
        )
        totals, carry = core(
            pieces, grads, shifted(tail, 1), conv_kernel, window, offsets, c * per_chunk, span
        )
        carried.append((totals, shifted(carry, -1)))
    results = []
    for c, (totals, carry) in enumerate(carried):
        outs = finish(totals, carry, conv_kernel, c * per_chunk, n_head, span)
        results.append([partner(outs[j], j) for j in range(n_head)])
    return unpack(results, n_head, n_chunks)


def solution(mesh):
    return jax.shard_map(
        per_device,
        mesh=mesh,
        in_specs=(
            P(("seq", "head"), None, None, None),
            P(("seq", "head"), None),
            P("head", None),
            P(),
            P(None, None, "head", None),
            P(),
            P(),
        ),
        out_specs=P(("seq", "head"), None, None, None),
        check_vma=False,
    )
```

```python
import functools
import math

import jax
import jax.numpy as jnp
from jax import lax
from jax.experimental import pallas as pl
from jax.experimental.pallas import tpu as pltpu
from jax.sharding import PartitionSpec as P

KW = 31
MASKB = 512
TILE = 128
PAD = 32
NEG = -1e30
F32 = jnp.float32
BF16 = jnp.bfloat16
MIB = 1024 * 1024
NT = (((1,), (1,)), ((), ()))
TN = (((0,), (0,)), ((), ()))


def call(kernel, mib, cost, **kw):
    estimate = pl.CostEstimate(
        flops=int(cost * 1e9), bytes_accessed=int(cost * 3e6), transcendentals=0
    )
    return pl.pallas_call(
        kernel,
        compiler_params=pltpu.CompilerParams(vmem_limit_bytes=mib * MIB),
        cost_estimate=estimate,
        **kw,
    )


def loop(count, body):
    if count <= 4:
        for i in range(count):
            body(i)
    else:
        lax.fori_loop(0, count, lambda i, c: (body(i), c)[1], 0)


def pack_kernel(n_head, n_chunks, src, *refs):
    near, far, stage = refs[: n_head // 2], refs[n_head // 2 : -1], refs[-1]
    local = src.shape[2] // n_head
    per_chunk = local // n_chunks
    me = lax.axis_index("head")
    stage[...] = jnp.swapaxes(src[:, 0], 0, 1)
    for j in range(n_head):
        first = jnp.bitwise_xor(me, j) * local
        for h in range(local):
            block = stage[first + h]
            if j < n_head // 2:
                near[j][0, h] = block
            else:
                at = (h // per_chunk) * (n_head // 2) + j - n_head // 2
                far[at][0, h % per_chunk] = block


def pack(qkv, n_head, n_chunks):
    tokens, parts, heads, dim = qkv.shape
    half = n_head // 2
    sizes = [heads // n_head] * half + [heads // n_head // n_chunks] * (half * n_chunks)
    outs = call(
        functools.partial(pack_kernel, n_head, n_chunks),
        8,
        2,
        grid=(parts,),
        in_specs=[pl.BlockSpec((tokens, 1, heads, dim), lambda p: (0, p, 0, 0))],
        out_specs=[pl.BlockSpec((1, size, tokens, dim), lambda p: (p, 0, 0, 0)) for size in sizes],
        out_shape=[jax.ShapeDtypeStruct((parts, size, tokens, dim), BF16) for size in sizes],
        scratch_shapes=[pltpu.VMEM((heads, tokens, dim), BF16)],
        name="pack",
    )(qkv)
    outs = list(outs)
    return outs[:half], [outs[half * (c + 1) : half * (c + 2)] for c in range(n_chunks)]


def unpack_kernel(n_head, n_chunks, *refs):
    srcs, out, stage = refs[:-2], refs[-2], refs[-1]
    heads = out.shape[2]
    local = heads // n_head
    per_chunk = local // n_chunks
    me = lax.axis_index("head")
    for j in range(n_head):
        first = jnp.bitwise_xor(me, j) * local
        for c in range(n_chunks):
            for h in range(per_chunk):
                stage[first + c * per_chunk + h] = srcs[c * n_head + j][0, h]
    out[:, 0] = jnp.swapaxes(stage[...], 0, 1)


def unpack(pieces, n_head, n_chunks):
    parts, per_chunk, tokens, dim = pieces[0][0].shape
    heads = per_chunk * n_chunks * n_head
    flat = [piece for chunk in pieces for piece in chunk]
    return call(
        functools.partial(unpack_kernel, n_head, n_chunks),
        8,
        2,
        grid=(parts,),
        in_specs=[pl.BlockSpec((1, per_chunk, tokens, dim), lambda p: (p, 0, 0, 0))] * len(flat),
        out_specs=pl.BlockSpec((tokens, 1, heads, dim), lambda p: (0, p, 0, 0)),
        out_shape=jax.ShapeDtypeStruct((tokens, parts, heads, dim), BF16),
        scratch_shapes=[pltpu.VMEM((heads, tokens, dim), BF16)],
        name="unpack",
    )(*flat)


def dequant_kernel(side, values, scales, weight):
    rows, width = values.shape
    first = lax.axis_index("head") * (rows // side)
    for r in range(rows // side):
        for c in range(width // side):
            block = values[r * side : (r + 1) * side, c * side : (c + 1) * side].astype(F32)
            block = block * scales[first + r, pl.program_id(0) * (width // side) + c]
            weight[c * side : (c + 1) * side, r * side : (r + 1) * side] = block.T.astype(BF16)


def dequantize(values, scales):
    rows, width = values.shape
    side = width // scales.shape[1]
    step = 4 * side
    return call(
        functools.partial(dequant_kernel, side),
        8,
        2,
        grid=(width // step,),
        in_specs=[
            pl.BlockSpec((rows, step), lambda i: (0, i)),
            pl.BlockSpec(memory_space=pltpu.SMEM),
        ],
        out_specs=pl.BlockSpec((step, rows), lambda i: (i, 0)),
        out_shape=jax.ShapeDtypeStruct((width, rows), BF16),
        name="dequant",
    )(values, scales)


def dattn_kernel(count, *refs):
    weight = refs[count]
    for grads, out in zip(refs[:count], refs[count + 1 :]):
        out[...] = jnp.dot(grads[...], weight[...], preferred_element_type=F32).astype(BF16)


def d_attn(pieces, weight):
    out = jax.ShapeDtypeStruct((pieces[0].shape[0], weight.shape[1]), BF16)
    return call(
        functools.partial(dattn_kernel, len(pieces)),
        12,
        1.5,
        out_shape=[out] * len(pieces),
        name="dattn",
    )(*pieces, weight)


def spread(totals, taps, head, p, first, rows):
    acc = jnp.zeros((rows, totals.shape[-1]), F32)
    for b in range(8):
        window_rows = totals[p, pl.ds(first + b, rows + 24), :]
        for a in range(4):
            tau = 8 * a + b
            if tau < KW:
                acc = acc + taps[tau, p, pl.ds(head, 1), :] * window_rows[8 * a : 8 * a + rows]
    return acc


def convolve(ext, taps, head, p, first, rows):
    acc = jnp.zeros((rows, ext.shape[-1]), F32)
    for b in range(8):
        window_rows = ext[p, pl.ds(first + 8 - b, rows + 24), :]
        for a in range(4):
            tau = 8 * a + b
            if tau < KW:
                at = 24 - 8 * a
                acc = acc + taps[tau, p, pl.ds(head, 1), :] * window_rows[at : at + rows]
    return acc.astype(BF16)


def steps(rows):
    return 112 if rows % 112 == 0 else PAD


def near_kernel(n_head, taps, *refs):
    pieces, mixed, ext = refs[: n_head // 2], *refs[n_head // 2 :]
    tokens = pieces[0].shape[2]
    half = tokens * len(pieces)
    me = lax.axis_index("head")
    head = pl.program_id(0)
    for j, piece in enumerate(pieces):
        start = pl.multiple_of(jnp.bitwise_xor(me % len(pieces), j) * tokens, tokens)
        for p in range(3):
            ext[p, pl.ds(start, tokens), :] = piece[p, 0].astype(F32)
    size = steps(half - PAD)
    blocks = (half - PAD) // size

    def block(i, c):
        first = pl.multiple_of(lax.rem(i, blocks) * size, 16)
        p = i // blocks
        mixed[p, 0, pl.ds(first, size), :] = convolve(ext, taps, head, p, first, size)
        return c

    lax.fori_loop(0, 3 * blocks, block, 0)


def conv_near(pieces, taps):
    parts, heads, tokens, dim = pieces[0].shape
    half = tokens * len(pieces)
    return call(
        functools.partial(near_kernel, 2 * len(pieces)),
        16,
        heads,
        grid=(heads,),
        in_specs=[pl.BlockSpec(taps.shape, lambda h: (0, 0, 0, 0))]
        + [pl.BlockSpec((parts, 1, tokens, dim), lambda h: (0, h, 0, 0))] * len(pieces),
        out_specs=pl.BlockSpec((parts, 1, half - PAD, dim), lambda h: (0, h, 0, 0)),
        out_shape=jax.ShapeDtypeStruct((parts, heads, half - PAD, dim), BF16),
        scratch_shapes=[pltpu.VMEM((parts, half, dim), F32)],
        name="conv_near",
    )(taps, *pieces)


def far_kernel(n_head, head0, taps, *refs):
    pieces, mixed, middle, first_rows, ext = refs[:n_head], *refs[n_head:]
    tokens = pieces[0].shape[2]
    half = tokens * n_head // 2
    me = lax.axis_index("head")
    head = head0 + pl.program_id(0)
    for j in range(n_head):
        start = pl.multiple_of(jnp.bitwise_xor(me, j) * tokens, tokens)
        for p in range(3):
            ext[p, pl.ds(start, tokens), :] = pieces[j][p, 0].astype(F32)
    size = steps(half - PAD)
    blocks = (half - PAD) // size
    base = jnp.where(me < n_head // 2, half, 0)

    def block(i, c):
        first = pl.multiple_of(lax.rem(i, blocks) * size, 16)
        p = i // blocks
        at = pl.multiple_of(base + first, 16)
        mixed[p, 0, pl.ds(first, size), :] = convolve(ext, taps, head, p, at, size)
        return c

    lax.fori_loop(0, 3 * blocks, block, 0)
    for p in range(3):
        middle[p, 0] = convolve(ext, taps, head, p, half - PAD, PAD)
        first_rows[p, 0] = ext[p, :PAD].astype(BF16)


def conv_far(near, far, taps, head0):
    n_head = len(near) + len(far)
    parts, heads, tokens, dim = far[0].shape
    half = tokens * n_head // 2
    sizes = (half - PAD, PAD, PAD)
    return call(
        functools.partial(far_kernel, n_head, head0),
        16,
        heads,
        grid=(heads,),
        in_specs=[pl.BlockSpec(taps.shape, lambda h: (0, 0, 0, 0))]
        + [pl.BlockSpec((parts, 1, tokens, dim), lambda h: (0, head0 + h, 0, 0))] * len(near)
        + [pl.BlockSpec((parts, 1, tokens, dim), lambda h: (0, h, 0, 0))] * len(far),
        out_specs=[pl.BlockSpec((parts, 1, rows, dim), lambda h: (0, h, 0, 0)) for rows in sizes],
        out_shape=[jax.ShapeDtypeStruct((parts, heads, rows, dim), BF16) for rows in sizes],
        scratch_shapes=[pltpu.VMEM((parts, 2 * half, dim), F32)],
        name="conv_far",
    )(taps, *near, *far)


def attn_kernel(n_head, head0, span, window, offsets, near, far, middle, first_rows, halo, taps, *refs):
    grads = refs[:n_head]
    totals_out, carry_out, ext, mixed, d_out = refs[n_head:]
    totals = totals_out.at[:, 0]
    tokens, dim = grads[0].shape
    seq_rows = tokens * n_head
    half = seq_rows // 2
    margin = span + PAD
    keys = span + TILE
    scale = 1.0 / math.sqrt(dim)
    me = lax.axis_index("head")
    seq_index = lax.axis_index("seq")
    head = head0 + pl.program_id(0)
    local = taps.shape[2]

    keep = seq_index > 0
    ext[1, :margin] = jnp.where(keep, halo[0, :margin].astype(F32), 0.0)
    ext[2, :margin] = jnp.where(keep, halo[0, margin : 2 * margin].astype(F32), 0.0)
    ext[0, span:margin] = jnp.where(keep, halo[0, 2 * margin :].astype(F32), 0.0)
    here = jnp.where(me < n_head // 2, 0, half)
    for p in range(3):
        ext[p, margin:] = first_rows[p, 0].astype(F32)
        mixed[p, pl.ds(pl.multiple_of(margin + here, PAD), half - PAD), :] = near[p, 0]
        mixed[p, pl.ds(pl.multiple_of(margin + half - here, PAD), half - PAD), :] = far[p, 0]
        mixed[p, span + half : margin + half] = middle[p, 0]
    mixed[0, span:margin] = convolve(ext, taps, head, 0, span, PAD)
    size = 5 * PAD if margin % (5 * PAD) == 0 else PAD
    for p in (1, 2):
        for first in range(0, margin, size):
            mixed[p, first : first + size] = convolve(ext, taps, head, p, first, size)
    for j in range(n_head):
        start = pl.multiple_of(jnp.bitwise_xor(me, j) * tokens, tokens)
        d_out[pl.ds(start, tokens), :] = grads[j][...]

    totals[1] = jnp.zeros(totals.shape[1:], F32)
    totals[2] = jnp.zeros(totals.shape[1:], F32)
    row = lax.broadcasted_iota(jnp.int32, (TILE, keys), 0)
    col = lax.broadcasted_iota(jnp.int32, (TILE, keys), 1)
    distance = row + span - col
    base = window[me * local + head]
    blocks = seq_rows // MASKB

    def attend(t):
        first = t * TILE
        reach = base + offsets[seq_index * blocks + first // MASKB]
        limit = jnp.minimum(reach, seq_index * seq_rows + first + row)
        allowed = (distance >= 0) & (distance <= limit)
        q = mixed[0, pl.ds(span + first, TILE), :]
        k = mixed[1, pl.ds(first, keys), :]
        v = mixed[2, pl.ds(first, keys), :]
        o = d_out[pl.ds(first, TILE), :]
        scores = lax.dot_general(q, k, NT, preferred_element_type=F32)
        d_prob = lax.dot_general(o, v, NT, preferred_element_type=F32)
        scores = jnp.where(allowed, scores, NEG)
        top = jnp.max(scores, axis=1, keepdims=True)
        exps = jnp.exp((scores - top) * scale)
        probs = exps * (1.0 / jnp.sum(exps, axis=1, keepdims=True))
        delta = jnp.sum(probs * d_prob, axis=1, keepdims=True)
        d_score = (probs * ((d_prob - delta) * scale)).astype(BF16)
        probs_b = probs.astype(BF16)
        totals[0, pl.ds(span + first, TILE), :] = jnp.dot(d_score, k, preferred_element_type=F32)
        at = pl.ds(first, keys)
        totals[1, at, :] += lax.dot_general(d_score, q, TN, preferred_element_type=F32)
        totals[2, at, :] += lax.dot_general(probs_b, o, TN, preferred_element_type=F32)

    loop(seq_rows // TILE, attend)

    carry_out[0, :span] = totals[1, :span].astype(BF16)
    carry_out[0, span : 2 * span] = totals[2, :span].astype(BF16)
    for p in range(3):
        at = 2 * span + p * PAD
        carry_out[0, at : at + PAD] = totals[p, span:margin].astype(BF16)


def attention(near, far_parts, halo, grads, taps, window, offsets, head0, span):
    parts, heads, rows, dim = far_parts[0].shape
    seq_rows = 2 * (rows + PAD)
    n_head = len(grads)
    tokens = seq_rows // n_head
    margin = span + PAD
    edge = 2 * span + 3 * PAD
    mine = lambda h: (0, h, 0, 0)
    return call(
        functools.partial(attn_kernel, n_head, head0, span),
        16,
        2.5 * heads,
        grid=(heads,),
        in_specs=[pl.BlockSpec(memory_space=pltpu.SMEM)] * 2
        + [
            pl.BlockSpec((parts, 1, rows, dim), lambda h: (0, head0 + h, 0, 0)),
            pl.BlockSpec((parts, 1, rows, dim), mine),
            pl.BlockSpec((parts, 1, PAD, dim), mine),
            pl.BlockSpec((parts, 1, PAD, dim), mine),
            pl.BlockSpec((1, 2 * margin + PAD, dim), lambda h: (h, 0, 0)),
            pl.BlockSpec(taps.shape, lambda h: (0, 0, 0, 0)),
        ]
        + [pl.BlockSpec((tokens, dim), lambda h: (0, head0 + h))] * n_head,
        out_specs=[
            pl.BlockSpec((parts, 1, span + seq_rows, dim), mine),
            pl.BlockSpec((1, edge, dim), lambda h: (h, 0, 0)),
        ],
        out_shape=[
            jax.ShapeDtypeStruct((parts, heads, span + seq_rows, dim), F32),
            jax.ShapeDtypeStruct((heads, edge, dim), BF16),
        ],
        scratch_shapes=[
            pltpu.VMEM((parts, margin + PAD, dim), F32),
            pltpu.VMEM((parts, span + seq_rows, dim), BF16),
            pltpu.VMEM((seq_rows, dim), BF16),
        ],
        name="attention",
    )(window, offsets, near, *far_parts, halo, taps, *grads)


def finish_kernel(n_head, head0, span, totals, carry, taps, *refs):
    outs, rows = refs[:-1], refs[-1]
    tokens = outs[0].shape[2]
    seq_rows = tokens * n_head
    me = lax.axis_index("head")
    head = head0 + pl.program_id(0)
    inner = lax.axis_index("seq") < lax.axis_size("seq") - 1

    rows[0, :seq_rows] = totals[0, 0, span:]
    for p in (1, 2):
        edge = seq_rows - span
        back = carry[0, (p - 1) * span : p * span].astype(F32)
        rows[p, :edge] = totals[p, 0, span:seq_rows]
        rows[p, edge:seq_rows] = totals[p, 0, seq_rows:] + jnp.where(inner, back, 0.0)
    for p in range(3):
        at = 2 * span + p * PAD
        rows[p, seq_rows:] = jnp.where(inner, carry[0, at : at + PAD].astype(F32), 0.0)
    for j in range(n_head):
        start = pl.multiple_of(jnp.bitwise_xor(me, j) * tokens, tokens)

        def part(p, c, j=j, start=start):
            outs[j][p, 0] = spread(rows, taps, head, p, start, tokens).astype(BF16)
            return c

        lax.fori_loop(0, 3, part, 0)


def finish(totals, carry, taps, head0, n_head, span):
    parts, heads, rows, dim = totals.shape
    seq_rows = rows - span
    tokens = seq_rows // n_head
    return call(
        functools.partial(finish_kernel, n_head, head0, span),
        16,
        2 * heads,
        grid=(heads,),
        in_specs=[
            pl.BlockSpec((parts, 1, rows, dim), lambda h: (0, h, 0, 0)),
            pl.BlockSpec((1, carry.shape[1], dim), lambda h: (h, 0, 0)),
            pl.BlockSpec(taps.shape, lambda h: (0, 0, 0, 0)),
        ],
        out_specs=[pl.BlockSpec((parts, 1, tokens, dim), lambda h: (0, h, 0, 0))] * n_head,
        out_shape=[jax.ShapeDtypeStruct((parts, heads, tokens, dim), BF16)] * n_head,
        scratch_shapes=[pltpu.VMEM((parts, seq_rows + PAD, dim), F32)],
        name="finish",
    )(totals, carry, taps)


def partner(value, j):
    if j == 0:
        return value
    size = lax.axis_size("head")
    return lax.ppermute(value, "head", [(i, i ^ j) for i in range(size)])


def shifted(value, by):
    length = lax.axis_size("seq")
    pairs = [(i, (i + by) % length) for i in range(length)]
    return lax.ppermute(value, "seq", pairs)


def tail_kernel(n_head, head0, span, *refs):
    pieces, out, sems = refs[:n_head], refs[n_head], refs[n_head + 1]
    tokens = pieces[0].shape[2]
    heads = out.shape[0]
    margin = span + PAD
    me = lax.axis_index("head")
    moves = []
    for p, rows, at in ((1, margin, 0), (2, margin, margin), (0, PAD, 2 * margin)):
        source = n_head - 1
        while rows > 0:
            take = min(rows, tokens)
            rows -= take
            moves.append((p, source, take, at + rows))
            source -= 1

    def move(i, j):
        p, _, take, at = moves[i]
        first = head0 if j < n_head // 2 else 0
        return pltpu.make_async_copy(
            pieces[j].at[p, first : first + heads, tokens - take :],
            out.at[:, at : at + take],
            sems.at[i],
        )

    for i, (_, source, _, _) in enumerate(moves):
        for j in range(n_head):
            pl.when(me == source ^ j)(lambda i=i, j=j: move(i, j).start())
    for i in range(len(moves)):
        move(i, 0).wait()


def tail_of(near, far, head0, span):
    pieces = list(near) + list(far)
    _, heads, tokens, dim = far[0].shape
    margin = span + PAD
    count = 2 * -(-margin // tokens) + 1
    return call(
        functools.partial(tail_kernel, len(pieces), head0, span),
        8,
        0.5,
        in_specs=[pl.BlockSpec(memory_space=pl.ANY)] * len(pieces),
        out_specs=pl.BlockSpec(memory_space=pl.ANY),
        out_shape=jax.ShapeDtypeStruct((heads, 2 * margin + PAD, dim), BF16),
        scratch_shapes=[pltpu.SemaphoreType.DMA((count,))],
        name="tail",
    )(*pieces)


def tied(*values):
    return lax.optimization_barrier(values)


def per_device(qkv_pre, grad_out, out_values, out_scales, conv_kernel, window, offsets):
    n_head = lax.axis_size("head")
    tokens, _, heads, dim = qkv_pre.shape
    local = heads // n_head
    n_chunks = 2 if local % 2 == 0 else 1
    per_chunk = local // n_chunks
    half = n_head // 2
    span = tokens * n_head // 4

    g_near = [partner(grad_out, j) for j in range(half)]
    g_far = partner(grad_out, half)
    near, far = pack(qkv_pre, n_head, n_chunks)
    near = [partner(near[j], j) for j in range(half)]
    far = [[partner(far[c][j], half + j) for j in range(half)] for c in range(n_chunks)]
    near, values, g_near = tied(near, out_values, g_near)
    weight = dequantize(values, out_scales)
    grads = list(d_attn(g_near, weight))
    near, grads = tied(near, grads)
    mixed_near = conv_near(near, conv_kernel)
    far[0], g_far, mixed_near = tied(far[0], g_far, mixed_near)

    def halo_of(c):
        tail = tail_of(near, far[c], c * per_chunk, span)
        far[c], tail = tied(far[c], tail)
        return shifted(tail, 1)

    halo = halo_of(0)
    g_rest = [partner(g_far, j) for j in range(1, half)]
    parts = conv_far(near, far[0], conv_kernel, 0)
    g_rest, parts = tied(g_rest, parts)
    grads += list(d_attn([g_far] + g_rest, weight))
    parts, grads, halo = tied(parts, grads, halo)
    held = []
    for c in range(n_chunks):
        if c + 1 < n_chunks:
            far[c + 1], halo, parts = tied(far[c + 1], halo, parts)
            later = halo_of(c + 1)
        totals, carry = attention(
            mixed_near, parts, halo, grads, conv_kernel, window, offsets, c * per_chunk, span
        )
        if c + 1 < n_chunks:
            halo, totals, carry, near = tied(later, totals, carry, near)
            parts = conv_far(near, far[c + 1], conv_kernel, (c + 1) * per_chunk)
        held.append((totals, shifted(carry, -1)))
    results = []
    held[0], last = tied(held[0], held[-1][0])
    for c in range(n_chunks):
        outs = finish(*held[c], conv_kernel, c * per_chunk, n_head, span)
        if c > 0:
            sent, outs = tied(results[c - 1][: half + 1], outs)
            results[c - 1][: half + 1] = sent
        if c + 1 < n_chunks:
            outs, totals = tied(outs, held[c + 1][0])
            held[c + 1] = (totals, held[c + 1][1])
        results.append([partner(outs[j], j) for j in range(n_head)])
    return unpack(results, n_head, n_chunks)


def solution(mesh):
    return jax.shard_map(
        per_device,
        mesh=mesh,
        in_specs=(
            P(("seq", "head"), None, None, None),
            P(("seq", "head"), None),
            P("head", None),
            P(),
            P(None, None, "head", None),
            P(),
            P(),
        ),
        out_specs=P(("seq", "head"), None, None, None),
        check_vma=False,
    )
```

```python
import functools
import math

import jax
import jax.numpy as jnp
from jax import lax
from jax.experimental import pallas as pl
from jax.experimental.pallas import tpu as pltpu
from jax.sharding import PartitionSpec as P

KW = 31
MASKB = 512
TILE = 128
PAD = 32
NEG = -1e30
F32 = jnp.float32
BF16 = jnp.bfloat16
MIB = 1024 * 1024
NT = (((1,), (1,)), ((), ()))
TN = (((0,), (0,)), ((), ()))


def call(kernel, mib, cost, **kw):
    estimate = pl.CostEstimate(
        flops=int(cost * 1e9), bytes_accessed=int(cost * 3e6), transcendentals=0
    )
    return pl.pallas_call(
        kernel,
        compiler_params=pltpu.CompilerParams(vmem_limit_bytes=mib * MIB),
        cost_estimate=estimate,
        **kw,
    )


def loop(count, body):
    if count <= 4:
        for i in range(count):
            body(i)
    else:
        lax.fori_loop(0, count, lambda i, c: (body(i), c)[1], 0)


def pack_kernel(n_head, n_chunks, src, *refs):
    near, far, stage = refs[: n_head // 2], refs[n_head // 2 : -1], refs[-1]
    local = src.shape[2] // n_head
    per_chunk = local // n_chunks
    me = lax.axis_index("head")
    stage[...] = jnp.swapaxes(src[:, 0], 0, 1)
    for j in range(n_head):
        first = jnp.bitwise_xor(me, j) * local
        for h in range(local):
            block = stage[first + h]
            if j < n_head // 2:
                near[j][0, h] = block
            else:
                at = (h // per_chunk) * (n_head // 2) + j - n_head // 2
                far[at][0, h % per_chunk] = block


def pack(qkv, n_head, n_chunks):
    tokens, parts, heads, dim = qkv.shape
    half = n_head // 2
    sizes = [heads // n_head] * half + [heads // n_head // n_chunks] * (half * n_chunks)
    outs = call(
        functools.partial(pack_kernel, n_head, n_chunks),
        8,
        2,
        grid=(parts,),
        in_specs=[pl.BlockSpec((tokens, 1, heads, dim), lambda p: (0, p, 0, 0))],
        out_specs=[pl.BlockSpec((1, size, tokens, dim), lambda p: (p, 0, 0, 0)) for size in sizes],
        out_shape=[jax.ShapeDtypeStruct((parts, size, tokens, dim), BF16) for size in sizes],
        scratch_shapes=[pltpu.VMEM((heads, tokens, dim), BF16)],
        name="pack",
    )(qkv)
    outs = list(outs)
    return outs[:half], [outs[half * (c + 1) : half * (c + 2)] for c in range(n_chunks)]


def unpack_kernel(n_head, n_chunks, *refs):
    srcs, out, stage = refs[:-2], refs[-2], refs[-1]
    heads = out.shape[2]
    local = heads // n_head
    per_chunk = local // n_chunks
    me = lax.axis_index("head")
    for j in range(n_head):
        first = jnp.bitwise_xor(me, j) * local
        for c in range(n_chunks):
            for h in range(per_chunk):
                stage[first + c * per_chunk + h] = srcs[c * n_head + j][0, h]
    out[:, 0] = jnp.swapaxes(stage[...], 0, 1)


def unpack(pieces, n_head, n_chunks):
    parts, per_chunk, tokens, dim = pieces[0][0].shape
    heads = per_chunk * n_chunks * n_head
    flat = [piece for chunk in pieces for piece in chunk]
    return call(
        functools.partial(unpack_kernel, n_head, n_chunks),
        8,
        2,
        grid=(parts,),
        in_specs=[pl.BlockSpec((1, per_chunk, tokens, dim), lambda p: (p, 0, 0, 0))] * len(flat),
        out_specs=pl.BlockSpec((tokens, 1, heads, dim), lambda p: (0, p, 0, 0)),
        out_shape=jax.ShapeDtypeStruct((tokens, parts, heads, dim), BF16),
        scratch_shapes=[pltpu.VMEM((heads, tokens, dim), BF16)],
        name="unpack",
    )(*flat)


def dequant_kernel(side, values, scales, weight):
    rows, width = values.shape
    first = lax.axis_index("head") * (rows // side)
    for r in range(rows // side):
        for c in range(width // side):
            block = values[r * side : (r + 1) * side, c * side : (c + 1) * side].astype(F32)
            block = block * scales[first + r, pl.program_id(0) * (width // side) + c]
            weight[c * side : (c + 1) * side, r * side : (r + 1) * side] = block.T.astype(BF16)


def dequantize(values, scales):
    rows, width = values.shape
    side = width // scales.shape[1]
    step = 4 * side
    return call(
        functools.partial(dequant_kernel, side),
        8,
        0.01,
        grid=(width // step,),
        in_specs=[
            pl.BlockSpec((rows, step), lambda i: (0, i)),
            pl.BlockSpec(memory_space=pltpu.SMEM),
        ],
        out_specs=pl.BlockSpec((step, rows), lambda i: (i, 0)),
        out_shape=jax.ShapeDtypeStruct((width, rows), BF16),
        name="dequant",
    )(values, scales)


def dattn_kernel(count, *refs):
    weight = refs[count]
    for grads, out in zip(refs[:count], refs[count + 1 :]):
        out[...] = jnp.dot(grads[...], weight[...], preferred_element_type=F32).astype(BF16)


def d_attn(pieces, weight):
    out = jax.ShapeDtypeStruct((pieces[0].shape[0], weight.shape[1]), BF16)
    return call(
        functools.partial(dattn_kernel, len(pieces)),
        12,
        0.01,
        out_shape=[out] * len(pieces),
        name="dattn",
    )(*pieces, weight)


def spread(totals, taps, head, p, first, rows):
    acc = jnp.zeros((rows, totals.shape[-1]), F32)
    for b in range(8):
        window_rows = totals[p, pl.ds(first + b, rows + 24), :]
        for a in range(4):
            tau = 8 * a + b
            if tau < KW:
                acc = acc + taps[tau, p, pl.ds(head, 1), :] * window_rows[8 * a : 8 * a + rows]
    return acc


def convolve(ext, taps, head, p, first, rows):
    acc = jnp.zeros((rows, ext.shape[-1]), F32)
    for b in range(8):
        window_rows = ext[p, pl.ds(first + 8 - b, rows + 24), :]
        for a in range(4):
            tau = 8 * a + b
            if tau < KW:
                at = 24 - 8 * a
                acc = acc + taps[tau, p, pl.ds(head, 1), :] * window_rows[at : at + rows]
    return acc.astype(BF16)


def steps(rows):
    return 112 if rows % 112 == 0 else PAD


def near_kernel(n_head, taps, *refs):
    pieces, mixed, ext = refs[: n_head // 2], *refs[n_head // 2 :]
    tokens = pieces[0].shape[2]
    half = tokens * len(pieces)
    me = lax.axis_index("head")
    head = pl.program_id(0)
    for j, piece in enumerate(pieces):
        start = pl.multiple_of(jnp.bitwise_xor(me % len(pieces), j) * tokens, tokens)
        for p in range(3):
            ext[p, pl.ds(start, tokens), :] = piece[p, 0].astype(F32)
    size = steps(half - PAD)
    blocks = (half - PAD) // size

    def block(i, c):
        first = pl.multiple_of(lax.rem(i, blocks) * size, 16)
        p = i // blocks
        mixed[p, 0, pl.ds(first, size), :] = convolve(ext, taps, head, p, first, size)
        return c

    lax.fori_loop(0, 3 * blocks, block, 0)


def conv_near(pieces, taps):
    parts, heads, tokens, dim = pieces[0].shape
    half = tokens * len(pieces)
    return call(
        functools.partial(near_kernel, 2 * len(pieces)),
        16,
        0.01,
        grid=(heads,),
        in_specs=[pl.BlockSpec(taps.shape, lambda h: (0, 0, 0, 0))]
        + [pl.BlockSpec((parts, 1, tokens, dim), lambda h: (0, h, 0, 0))] * len(pieces),
        out_specs=pl.BlockSpec((parts, 1, half - PAD, dim), lambda h: (0, h, 0, 0)),
        out_shape=jax.ShapeDtypeStruct((parts, heads, half - PAD, dim), BF16),
        scratch_shapes=[pltpu.VMEM((parts, half, dim), F32)],
        name="conv_near",
    )(taps, *pieces)


def far_kernel(n_head, head0, taps, *refs):
    pieces, mixed, middle, first_rows, ext = refs[:n_head], *refs[n_head:]
    tokens = pieces[0].shape[2]
    half = tokens * n_head // 2
    me = lax.axis_index("head")
    head = head0 + pl.program_id(0)
    for j in range(n_head):
        start = pl.multiple_of(jnp.bitwise_xor(me, j) * tokens, tokens)
        for p in range(3):
            ext[p, pl.ds(start, tokens), :] = pieces[j][p, 0].astype(F32)
    size = steps(half - PAD)
    blocks = (half - PAD) // size
    base = jnp.where(me < n_head // 2, half, 0)

    def block(i, c):
        first = pl.multiple_of(lax.rem(i, blocks) * size, 16)
        p = i // blocks
        at = pl.multiple_of(base + first, 16)
        mixed[p, 0, pl.ds(first, size), :] = convolve(ext, taps, head, p, at, size)
        return c

    lax.fori_loop(0, 3 * blocks, block, 0)
    for p in range(3):
        middle[p, 0] = convolve(ext, taps, head, p, half - PAD, PAD)
        first_rows[p, 0] = ext[p, :PAD].astype(BF16)


def conv_far(near, far, taps, head0):
    n_head = len(near) + len(far)
    parts, heads, tokens, dim = far[0].shape
    half = tokens * n_head // 2
    sizes = (half - PAD, PAD, PAD)
    return call(
        functools.partial(far_kernel, n_head, head0),
        16,
        0.01,
        grid=(heads,),
        in_specs=[pl.BlockSpec(taps.shape, lambda h: (0, 0, 0, 0))]
        + [pl.BlockSpec((parts, 1, tokens, dim), lambda h: (0, head0 + h, 0, 0))] * len(near)
        + [pl.BlockSpec((parts, 1, tokens, dim), lambda h: (0, h, 0, 0))] * len(far),
        out_specs=[pl.BlockSpec((parts, 1, rows, dim), lambda h: (0, h, 0, 0)) for rows in sizes],
        out_shape=[jax.ShapeDtypeStruct((parts, heads, rows, dim), BF16) for rows in sizes],
        scratch_shapes=[pltpu.VMEM((parts, 2 * half, dim), F32)],
        name="conv_far",
    )(taps, *near, *far)


def attn_kernel(n_head, head0, span, window, offsets, near, far, middle, first_rows, halo, taps, *refs):
    grads = refs[:n_head]
    totals_out, carry_out, ext, mixed, d_out = refs[n_head:]
    totals = totals_out.at[:, 0]
    tokens, dim = grads[0].shape
    seq_rows = tokens * n_head
    half = seq_rows // 2
    margin = span + PAD
    keys = span + TILE
    scale = 1.0 / math.sqrt(dim)
    me = lax.axis_index("head")
    seq_index = lax.axis_index("seq")
    head = head0 + pl.program_id(0)
    local = taps.shape[2]

    keep = seq_index > 0
    ext[1, :margin] = jnp.where(keep, halo[0, :margin].astype(F32), 0.0)
    ext[2, :margin] = jnp.where(keep, halo[0, margin : 2 * margin].astype(F32), 0.0)
    ext[0, span:margin] = jnp.where(keep, halo[0, 2 * margin :].astype(F32), 0.0)
    here = jnp.where(me < n_head // 2, 0, half)
    for p in range(3):
        ext[p, margin:] = first_rows[p, 0].astype(F32)
        mixed[p, pl.ds(pl.multiple_of(margin + here, PAD), half - PAD), :] = near[p, 0]
        mixed[p, pl.ds(pl.multiple_of(margin + half - here, PAD), half - PAD), :] = far[p, 0]
        mixed[p, span + half : margin + half] = middle[p, 0]
    mixed[0, span:margin] = convolve(ext, taps, head, 0, span, PAD)
    size = 5 * PAD if margin % (5 * PAD) == 0 else PAD
    for p in (1, 2):
        for first in range(0, margin, size):
            mixed[p, first : first + size] = convolve(ext, taps, head, p, first, size)
    for j in range(n_head):
        start = pl.multiple_of(jnp.bitwise_xor(me, j) * tokens, tokens)
        d_out[pl.ds(start, tokens), :] = grads[j][...]

    totals[1] = jnp.zeros(totals.shape[1:], F32)
    totals[2] = jnp.zeros(totals.shape[1:], F32)
    row = lax.broadcasted_iota(jnp.int32, (TILE, keys), 0)
    col = lax.broadcasted_iota(jnp.int32, (TILE, keys), 1)
    distance = row + span - col
    base = window[me * local + head]
    blocks = seq_rows // MASKB

    def attend(tiles):
        firsts = [t * TILE for t in tiles]
        q = [mixed[0, pl.ds(span + first, TILE), :] for first in firsts]
        k = [mixed[1, pl.ds(first, keys), :] for first in firsts]
        v = [mixed[2, pl.ds(first, keys), :] for first in firsts]
        o = [d_out[pl.ds(first, TILE), :] for first in firsts]
        every = range(len(firsts))
        scores = [lax.dot_general(q[i], k[i], NT, preferred_element_type=F32) for i in every]
        d_prob = [lax.dot_general(o[i], v[i], NT, preferred_element_type=F32) for i in every]
        for i, first in enumerate(firsts):
            reach = base + offsets[seq_index * blocks + first // MASKB]
            limit = jnp.minimum(reach, seq_index * seq_rows + first + row)
            scores[i] = jnp.where((distance >= 0) & (distance <= limit), scores[i], NEG)
        top = [jnp.max(scores[i], axis=1, keepdims=True) for i in every]
        exps = [jnp.exp((scores[i] - top[i]) * scale) for i in every]
        part = [1.0 / jnp.sum(exps[i], axis=1, keepdims=True) for i in every]
        probs = [exps[i] * part[i] for i in every]
        delta = [jnp.sum(probs[i] * d_prob[i], axis=1, keepdims=True) for i in every]
        d_score = [(probs[i] * ((d_prob[i] - delta[i]) * scale)).astype(BF16) for i in every]
        for i, first in enumerate(firsts):
            at = pl.ds(first, keys)
            totals[0, pl.ds(span + first, TILE), :] = jnp.dot(d_score[i], k[i], preferred_element_type=F32)
            totals[1, at, :] += lax.dot_general(d_score[i], q[i], TN, preferred_element_type=F32)
            totals[2, at, :] += lax.dot_general(
                probs[i].astype(BF16), o[i], TN, preferred_element_type=F32
            )

    count = seq_rows // TILE
    group = 4 if count % 4 == 0 else 1
    loop(count // group, lambda i: attend([i * group + n for n in range(group)]))

    carry_out[0, :span] = totals[1, :span].astype(BF16)
    carry_out[0, span : 2 * span] = totals[2, :span].astype(BF16)
    for p in range(3):
        at = 2 * span + p * PAD
        carry_out[0, at : at + PAD] = totals[p, span:margin].astype(BF16)


def attention(near, far_parts, halo, grads, taps, window, offsets, head0, span):
    parts, heads, rows, dim = far_parts[0].shape
    seq_rows = 2 * (rows + PAD)
    n_head = len(grads)
    tokens = seq_rows // n_head
    margin = span + PAD
    edge = 2 * span + 3 * PAD
    mine = lambda h: (0, h, 0, 0)
    return call(
        functools.partial(attn_kernel, n_head, head0, span),
        16,
        0.01,
        grid=(heads,),
        in_specs=[pl.BlockSpec(memory_space=pltpu.SMEM)] * 2
        + [
            pl.BlockSpec((parts, 1, rows, dim), lambda h: (0, head0 + h, 0, 0)),
            pl.BlockSpec((parts, 1, rows, dim), mine),
            pl.BlockSpec((parts, 1, PAD, dim), mine),
            pl.BlockSpec((parts, 1, PAD, dim), mine),
            pl.BlockSpec((1, 2 * margin + PAD, dim), lambda h: (h, 0, 0)),
            pl.BlockSpec(taps.shape, lambda h: (0, 0, 0, 0)),
        ]
        + [pl.BlockSpec((tokens, dim), lambda h: (0, head0 + h))] * n_head,
        out_specs=[
            pl.BlockSpec((parts, 1, span + seq_rows, dim), mine),
            pl.BlockSpec((1, edge, dim), lambda h: (h, 0, 0)),
        ],
        out_shape=[
            jax.ShapeDtypeStruct((parts, heads, span + seq_rows, dim), F32),
            jax.ShapeDtypeStruct((heads, edge, dim), BF16),
        ],
        scratch_shapes=[
            pltpu.VMEM((parts, margin + PAD, dim), F32),
            pltpu.VMEM((parts, span + seq_rows, dim), BF16),
            pltpu.VMEM((seq_rows, dim), BF16),
        ],
        name="attention",
    )(window, offsets, near, *far_parts, halo, taps, *grads)


def finish_kernel(n_head, head0, span, totals, carry, taps, *refs):
    outs, rows = refs[:-1], refs[-1]
    tokens = outs[0].shape[2]
    seq_rows = tokens * n_head
    me = lax.axis_index("head")
    head = head0 + pl.program_id(0)
    inner = lax.axis_index("seq") < lax.axis_size("seq") - 1

    rows[0, :seq_rows] = totals[0, 0, span:]
    for p in (1, 2):
        edge = seq_rows - span
        back = carry[0, (p - 1) * span : p * span].astype(F32)
        rows[p, :edge] = totals[p, 0, span:seq_rows]
        rows[p, edge:seq_rows] = totals[p, 0, seq_rows:] + jnp.where(inner, back, 0.0)
    for p in range(3):
        at = 2 * span + p * PAD
        rows[p, seq_rows:] = jnp.where(inner, carry[0, at : at + PAD].astype(F32), 0.0)
    for j in range(n_head):
        start = pl.multiple_of(jnp.bitwise_xor(me, j) * tokens, tokens)

        def part(p, c, j=j, start=start):
            outs[j][p, 0] = spread(rows, taps, head, p, start, tokens).astype(BF16)
            return c

        lax.fori_loop(0, 3, part, 0)


def finish(totals, carry, taps, head0, n_head, span):
    parts, heads, rows, dim = totals.shape
    seq_rows = rows - span
    tokens = seq_rows // n_head
    return call(
        functools.partial(finish_kernel, n_head, head0, span),
        16,
        2 * heads,
        grid=(heads,),
        in_specs=[
            pl.BlockSpec((parts, 1, rows, dim), lambda h: (0, h, 0, 0)),
            pl.BlockSpec((1, carry.shape[1], dim), lambda h: (h, 0, 0)),
            pl.BlockSpec(taps.shape, lambda h: (0, 0, 0, 0)),
        ],
        out_specs=[pl.BlockSpec((parts, 1, tokens, dim), lambda h: (0, h, 0, 0))] * n_head,
        out_shape=[jax.ShapeDtypeStruct((parts, heads, tokens, dim), BF16)] * n_head,
        scratch_shapes=[pltpu.VMEM((parts, seq_rows + PAD, dim), F32)],
        name="finish",
    )(totals, carry, taps)


def partner(value, j):
    if j == 0:
        return value
    size = lax.axis_size("head")
    return lax.ppermute(value, "head", [(i, i ^ j) for i in range(size)])


def shifted(value, by):
    length = lax.axis_size("seq")
    pairs = [(i, (i + by) % length) for i in range(length)]
    return lax.ppermute(value, "seq", pairs)


def tail_kernel(n_head, head0, span, *refs):
    pieces, out, sems = refs[:n_head], refs[n_head], refs[n_head + 1]
    tokens = pieces[0].shape[2]
    heads = out.shape[0]
    margin = span + PAD
    me = lax.axis_index("head")
    moves = []
    for p, rows, at in ((1, margin, 0), (2, margin, margin), (0, PAD, 2 * margin)):
        source = n_head - 1
        while rows > 0:
            take = min(rows, tokens)
            rows -= take
            moves.append((p, source, take, at + rows))
            source -= 1

    def move(i, j):
        p, _, take, at = moves[i]
        first = head0 if j < n_head // 2 else 0
        return pltpu.make_async_copy(
            pieces[j].at[p, first : first + heads, tokens - take :],
            out.at[:, at : at + take],
            sems.at[i],
        )

    for i, (_, source, _, _) in enumerate(moves):
        for j in range(n_head):
            pl.when(me == source ^ j)(lambda i=i, j=j: move(i, j).start())
    for i in range(len(moves)):
        move(i, 0).wait()


def tail_of(near, far, head0, span):
    pieces = list(near) + list(far)
    _, heads, tokens, dim = far[0].shape
    margin = span + PAD
    count = 2 * -(-margin // tokens) + 1
    return call(
        functools.partial(tail_kernel, len(pieces), head0, span),
        8,
        0.5,
        in_specs=[pl.BlockSpec(memory_space=pl.ANY)] * len(pieces),
        out_specs=pl.BlockSpec(memory_space=pl.ANY),
        out_shape=jax.ShapeDtypeStruct((heads, 2 * margin + PAD, dim), BF16),
        scratch_shapes=[pltpu.SemaphoreType.DMA((count,))],
        name="tail",
    )(*pieces)


def tied(*values):
    return lax.optimization_barrier(values)


def per_device(qkv_pre, grad_out, out_values, out_scales, conv_kernel, window, offsets):
    n_head = lax.axis_size("head")
    tokens, _, heads, dim = qkv_pre.shape
    local = heads // n_head
    n_chunks = 2 if local % 2 == 0 else 1
    per_chunk = local // n_chunks
    half = n_head // 2
    span = tokens * n_head // 4

    g_near = [partner(grad_out, j) for j in range(half)]
    g_far = partner(grad_out, half)
    near, far = pack(qkv_pre, n_head, n_chunks)
    near = [partner(near[j], j) for j in range(half)]
    far = [[partner(far[c][j], half + j) for j in range(half)] for c in range(n_chunks)]
    near, values, g_near = tied(near, out_values, g_near)
    weight = dequantize(values, out_scales)
    grads = list(d_attn(g_near, weight))
    near, grads = tied(near, grads)
    mixed_near = conv_near(near, conv_kernel)
    g_far, mixed_near = tied(g_far, mixed_near)
    far[0], g_far, mixed_near = tied(far[0], g_far, mixed_near)
    g_rest = [partner(g_far, j) for j in range(1, half)]

    halos, parts = [], []
    for c in range(n_chunks):
        if c > 0:
            far[c], parts, grads = tied(far[c], parts, grads)
        tail = tail_of(near, far[c], c * per_chunk, span)
        far[c], tail = tied(far[c], tail)
        halos.append(shifted(tail, 1))
        parts.append(conv_far(near, far[c], conv_kernel, c * per_chunk))
        if c == 0:
            g_rest, parts[0] = tied(g_rest, parts[0])
            grads += list(d_attn([g_far] + g_rest, weight))

    held = []
    parts, grads, halos[0] = tied(parts, grads, halos[0])
    for c in range(n_chunks):
        totals, carry = attention(
            mixed_near, parts[c], halos[c], grads, conv_kernel, window, offsets, c * per_chunk, span
        )
        if c + 1 < n_chunks:
            halos[c + 1], totals, carry = tied(halos[c + 1], totals, carry)
        held.append((totals, shifted(carry, -1)))
    results = []
    held[0], last = tied(held[0], held[-1][0])
    for c in range(n_chunks):
        outs = finish(*held[c], conv_kernel, c * per_chunk, n_head, span)
        if c > 0:
            sent, outs = tied(results[c - 1][: half + 1], outs)
            results[c - 1][: half + 1] = sent
        if c + 1 < n_chunks:
            outs, totals = tied(outs, held[c + 1][0])
            held[c + 1] = (totals, held[c + 1][1])
        results.append([partner(outs[j], j) for j in range(n_head)])
    return unpack(results, n_head, n_chunks)


def solution(mesh):
    return jax.shard_map(
        per_device,
        mesh=mesh,
        in_specs=(
            P(("seq", "head"), None, None, None),
            P(("seq", "head"), None),
            P("head", None),
            P(),
            P(None, None, "head", None),
            P(),
            P(),
        ),
        out_specs=P(("seq", "head"), None, None, None),
        check_vma=False,
    )
```

```python
import functools
import math

import jax
import jax.numpy as jnp
from jax import lax
from jax.experimental import pallas as pl
from jax.experimental.pallas import tpu as pltpu
from jax.sharding import PartitionSpec as P

KW = 31
MASKB = 512
TILE = 128
PAD = 32
NEG = -1e30
F32 = jnp.float32
BF16 = jnp.bfloat16
MIB = 1024 * 1024
NT = (((1,), (1,)), ((), ()))
TN = (((0,), (0,)), ((), ()))


def call(kernel, mib, cost, **kw):
    estimate = pl.CostEstimate(
        flops=int(cost * 1e9), bytes_accessed=int(cost * 3e6), transcendentals=0
    )
    return pl.pallas_call(
        kernel,
        compiler_params=pltpu.CompilerParams(vmem_limit_bytes=mib * MIB),
        cost_estimate=estimate,
        **kw,
    )


def loop(count, body):
    if count <= 4:
        for i in range(count):
            body(i)
    else:
        lax.fori_loop(0, count, lambda i, c: (body(i), c)[1], 0)


def pack_kernel(n_head, n_chunks, src, *refs):
    near, far, stage = refs[: n_head // 2], refs[n_head // 2 : -1], refs[-1]
    local = src.shape[2] // n_head
    per_chunk = local // n_chunks
    me = lax.axis_index("head")
    stage[...] = jnp.swapaxes(src[:, 0], 0, 1)
    for j in range(n_head):
        first = jnp.bitwise_xor(me, j) * local
        for h in range(local):
            block = stage[first + h]
            if j < n_head // 2:
                near[j][0, h] = block
            else:
                at = (h // per_chunk) * (n_head // 2) + j - n_head // 2
                far[at][0, h % per_chunk] = block


def pack(qkv, n_head, n_chunks):
    tokens, parts, heads, dim = qkv.shape
    half = n_head // 2
    sizes = [heads // n_head] * half + [heads // n_head // n_chunks] * (half * n_chunks)
    outs = call(
        functools.partial(pack_kernel, n_head, n_chunks),
        8,
        2,
        grid=(parts,),
        in_specs=[pl.BlockSpec((tokens, 1, heads, dim), lambda p: (0, p, 0, 0))],
        out_specs=[pl.BlockSpec((1, size, tokens, dim), lambda p: (p, 0, 0, 0)) for size in sizes],
        out_shape=[jax.ShapeDtypeStruct((parts, size, tokens, dim), BF16) for size in sizes],
        scratch_shapes=[pltpu.VMEM((heads, tokens, dim), BF16)],
        name="pack",
    )(qkv)
    outs = list(outs)
    return outs[:half], [outs[half * (c + 1) : half * (c + 2)] for c in range(n_chunks)]


def unpack_kernel(n_head, n_chunks, *refs):
    srcs, out, stage = refs[:-2], refs[-2], refs[-1]
    heads = out.shape[2]
    local = heads // n_head
    per_chunk = local // n_chunks
    me = lax.axis_index("head")
    for j in range(n_head):
        first = jnp.bitwise_xor(me, j) * local
        for c in range(n_chunks):
            for h in range(per_chunk):
                stage[first + c * per_chunk + h] = srcs[c * n_head + j][0, h]
    out[:, 0] = jnp.swapaxes(stage[...], 0, 1)


def unpack(pieces, n_head, n_chunks):
    parts, per_chunk, tokens, dim = pieces[0][0].shape
    heads = per_chunk * n_chunks * n_head
    flat = [piece for chunk in pieces for piece in chunk]
    return call(
        functools.partial(unpack_kernel, n_head, n_chunks),
        8,
        2,
        grid=(parts,),
        in_specs=[pl.BlockSpec((1, per_chunk, tokens, dim), lambda p: (p, 0, 0, 0))] * len(flat),
        out_specs=pl.BlockSpec((tokens, 1, heads, dim), lambda p: (0, p, 0, 0)),
        out_shape=jax.ShapeDtypeStruct((tokens, parts, heads, dim), BF16),
        scratch_shapes=[pltpu.VMEM((heads, tokens, dim), BF16)],
        name="unpack",
    )(*flat)


def dequant_kernel(side, values, scales, weight):
    rows, width = values.shape
    first = lax.axis_index("head") * (rows // side)
    for r in range(rows // side):
        for c in range(width // side):
            block = values[r * side : (r + 1) * side, c * side : (c + 1) * side].astype(F32)
            block = block * scales[first + r, pl.program_id(0) * (width // side) + c]
            weight[c * side : (c + 1) * side, r * side : (r + 1) * side] = block.T.astype(BF16)


def dequantize(values, scales):
    rows, width = values.shape
    side = width // scales.shape[1]
    step = 4 * side
    return call(
        functools.partial(dequant_kernel, side),
        8,
        0.01,
        grid=(width // step,),
        in_specs=[
            pl.BlockSpec((rows, step), lambda i: (0, i)),
            pl.BlockSpec(memory_space=pltpu.SMEM),
        ],
        out_specs=pl.BlockSpec((step, rows), lambda i: (i, 0)),
        out_shape=jax.ShapeDtypeStruct((width, rows), BF16),
        name="dequant",
    )(values, scales)


def dattn_kernel(count, *refs):
    weight = refs[count]
    for grads, out in zip(refs[:count], refs[count + 1 :]):
        out[...] = jnp.dot(grads[...], weight[...], preferred_element_type=F32).astype(BF16)


def d_attn(pieces, weight):
    out = jax.ShapeDtypeStruct((pieces[0].shape[0], weight.shape[1]), BF16)
    return call(
        functools.partial(dattn_kernel, len(pieces)),
        12,
        0.01,
        out_shape=[out] * len(pieces),
        name="dattn",
    )(*pieces, weight)


def weighted(ref, taps, head, p, start, rows, place):
    acc = None
    for b in range(8):
        window_rows = ref[p, pl.ds(start(b), rows + 24), :]
        terms = [
            taps[8 * a + b, p, pl.ds(head, 1), :] * window_rows[place(a) : place(a) + rows]
            for a in range(4)
            if 8 * a + b < KW
        ]
        while len(terms) > 1:
            terms = [sum(terms[i + 1 : i + 2], terms[i]) for i in range(0, len(terms), 2)]
        acc = terms[0] if acc is None else acc + terms[0]
    return acc


def spread(totals, taps, head, p, first, rows):
    return weighted(totals, taps, head, p, lambda b: first + b, rows, lambda a: 8 * a)


def convolve(ext, taps, head, p, first, rows):
    start = lambda b: first + 8 - b
    return weighted(ext, taps, head, p, start, rows, lambda a: 24 - 8 * a).astype(BF16)


def steps(rows):
    return 112 if rows % 112 == 0 else PAD


def near_kernel(n_head, taps, *refs):
    pieces, mixed, ext = refs[: n_head // 2], *refs[n_head // 2 :]
    tokens = pieces[0].shape[2]
    half = tokens * len(pieces)
    me = lax.axis_index("head")
    head = pl.program_id(0)
    for j, piece in enumerate(pieces):
        start = pl.multiple_of(jnp.bitwise_xor(me % len(pieces), j) * tokens, tokens)
        for p in range(3):
            ext[p, pl.ds(start, tokens), :] = piece[p, 0].astype(F32)
    size = steps(half - PAD)
    blocks = (half - PAD) // size

    def block(i, c):
        first = pl.multiple_of(lax.rem(i, blocks) * size, 16)
        p = i // blocks
        mixed[p, 0, pl.ds(first, size), :] = convolve(ext, taps, head, p, first, size)
        return c

    lax.fori_loop(0, 3 * blocks, block, 0)


def conv_near(pieces, taps):
    parts, heads, tokens, dim = pieces[0].shape
    half = tokens * len(pieces)
    return call(
        functools.partial(near_kernel, 2 * len(pieces)),
        16,
        0.01,
        grid=(heads,),
        in_specs=[pl.BlockSpec(taps.shape, lambda h: (0, 0, 0, 0))]
        + [pl.BlockSpec((parts, 1, tokens, dim), lambda h: (0, h, 0, 0))] * len(pieces),
        out_specs=pl.BlockSpec((parts, 1, half - PAD, dim), lambda h: (0, h, 0, 0)),
        out_shape=jax.ShapeDtypeStruct((parts, heads, half - PAD, dim), BF16),
        scratch_shapes=[pltpu.VMEM((parts, half, dim), F32)],
        name="conv_near",
    )(taps, *pieces)


def far_kernel(n_head, head0, taps, *refs):
    pieces, mixed, middle, first_rows, ext = refs[:n_head], *refs[n_head:]
    tokens = pieces[0].shape[2]
    half = tokens * n_head // 2
    me = lax.axis_index("head")
    head = head0 + pl.program_id(0)
    for j in range(n_head):
        start = pl.multiple_of(jnp.bitwise_xor(me, j) * tokens, tokens)
        for p in range(3):
            ext[p, pl.ds(start, tokens), :] = pieces[j][p, 0].astype(F32)
    size = steps(half - PAD)
    blocks = (half - PAD) // size
    base = jnp.where(me < n_head // 2, half, 0)

    def block(i, c):
        first = pl.multiple_of(lax.rem(i, blocks) * size, 16)
        p = i // blocks
        at = pl.multiple_of(base + first, 16)
        mixed[p, 0, pl.ds(first, size), :] = convolve(ext, taps, head, p, at, size)
        return c

    lax.fori_loop(0, 3 * blocks, block, 0)
    for p in range(3):
        middle[p, 0] = convolve(ext, taps, head, p, half - PAD, PAD)
        first_rows[p, 0] = ext[p, :PAD].astype(BF16)


def conv_far(near, far, taps, head0):
    n_head = len(near) + len(far)
    parts, heads, tokens, dim = far[0].shape
    half = tokens * n_head // 2
    sizes = (half - PAD, PAD, PAD)
    return call(
        functools.partial(far_kernel, n_head, head0),
        16,
        0.01,
        grid=(heads,),
        in_specs=[pl.BlockSpec(taps.shape, lambda h: (0, 0, 0, 0))]
        + [pl.BlockSpec((parts, 1, tokens, dim), lambda h: (0, head0 + h, 0, 0))] * len(near)
        + [pl.BlockSpec((parts, 1, tokens, dim), lambda h: (0, h, 0, 0))] * len(far),
        out_specs=[pl.BlockSpec((parts, 1, rows, dim), lambda h: (0, h, 0, 0)) for rows in sizes],
        out_shape=[jax.ShapeDtypeStruct((parts, heads, rows, dim), BF16) for rows in sizes],
        scratch_shapes=[pltpu.VMEM((parts, 2 * half, dim), F32)],
        name="conv_far",
    )(taps, *near, *far)


def attn_kernel(n_head, head0, span, window, offsets, near, far, middle, first_rows, halo, taps, *refs):
    grads = refs[:n_head]
    totals_out, carry_out, ext, mixed, d_out = refs[n_head:]
    totals = totals_out.at[:, 0]
    tokens, dim = grads[0].shape
    seq_rows = tokens * n_head
    half = seq_rows // 2
    margin = span + PAD
    keys = span + TILE
    scale = 1.0 / math.sqrt(dim)
    me = lax.axis_index("head")
    seq_index = lax.axis_index("seq")
    head = head0 + pl.program_id(0)
    local = taps.shape[2]

    keep = seq_index > 0
    ext[1, :margin] = jnp.where(keep, halo[0, :margin].astype(F32), 0.0)
    ext[2, :margin] = jnp.where(keep, halo[0, margin : 2 * margin].astype(F32), 0.0)
    ext[0, span:margin] = jnp.where(keep, halo[0, 2 * margin :].astype(F32), 0.0)
    here = jnp.where(me < n_head // 2, 0, half)
    for p in range(3):
        ext[p, margin:] = first_rows[p, 0].astype(F32)
        mixed[p, pl.ds(pl.multiple_of(margin + here, PAD), half - PAD), :] = near[p, 0]
        mixed[p, pl.ds(pl.multiple_of(margin + half - here, PAD), half - PAD), :] = far[p, 0]
        mixed[p, span + half : margin + half] = middle[p, 0]
    mixed[0, span:margin] = convolve(ext, taps, head, 0, span, PAD)
    size = 5 * PAD if margin % (5 * PAD) == 0 else PAD
    for p in (1, 2):
        for first in range(0, margin, size):
            mixed[p, first : first + size] = convolve(ext, taps, head, p, first, size)
    for j in range(n_head):
        start = pl.multiple_of(jnp.bitwise_xor(me, j) * tokens, tokens)
        d_out[pl.ds(start, tokens), :] = grads[j][...]

    totals[1] = jnp.zeros(totals.shape[1:], F32)
    totals[2] = jnp.zeros(totals.shape[1:], F32)
    row = lax.broadcasted_iota(jnp.int32, (TILE, keys), 0)
    col = lax.broadcasted_iota(jnp.int32, (TILE, keys), 1)
    distance = row + span - col
    base = window[me * local + head]
    blocks = seq_rows // MASKB

    def attend(tiles):
        firsts = [t * TILE for t in tiles]
        q = [mixed[0, pl.ds(span + first, TILE), :] for first in firsts]
        k = [mixed[1, pl.ds(first, keys), :] for first in firsts]
        v = [mixed[2, pl.ds(first, keys), :] for first in firsts]
        o = [d_out[pl.ds(first, TILE), :] for first in firsts]
        every = range(len(firsts))
        scores = [lax.dot_general(q[i], k[i], NT, preferred_element_type=F32) for i in every]
        d_prob = [lax.dot_general(o[i], v[i], NT, preferred_element_type=F32) for i in every]
        for i, first in enumerate(firsts):
            reach = base + offsets[seq_index * blocks + first // MASKB]
            limit = jnp.minimum(reach, seq_index * seq_rows + first + row)
            scores[i] = jnp.where((distance >= 0) & (distance <= limit), scores[i], NEG)
        top = [jnp.max(scores[i], axis=1, keepdims=True) for i in every]
        exps = [jnp.exp((scores[i] - top[i]) * scale) for i in every]
        part = [1.0 / jnp.sum(exps[i], axis=1, keepdims=True) for i in every]
        probs = [exps[i] * part[i] for i in every]
        delta = [jnp.sum(probs[i] * d_prob[i], axis=1, keepdims=True) for i in every]
        d_score = [(probs[i] * ((d_prob[i] - delta[i]) * scale)).astype(BF16) for i in every]
        for i, first in enumerate(firsts):
            at = pl.ds(first, keys)
            totals[0, pl.ds(span + first, TILE), :] = jnp.dot(d_score[i], k[i], preferred_element_type=F32)
            totals[1, at, :] += lax.dot_general(d_score[i], q[i], TN, preferred_element_type=F32)
            totals[2, at, :] += lax.dot_general(
                probs[i].astype(BF16), o[i], TN, preferred_element_type=F32
            )

    count = seq_rows // TILE
    group = 4 if count % 4 == 0 else 1
    loop(count // group, lambda i: attend([i * group + n for n in range(group)]))

    carry_out[0, :span] = totals[1, :span].astype(BF16)
    carry_out[0, span : 2 * span] = totals[2, :span].astype(BF16)
    for p in range(3):
        at = 2 * span + p * PAD
        carry_out[0, at : at + PAD] = totals[p, span:margin].astype(BF16)


def attention(near, far_parts, halo, grads, taps, window, offsets, head0, span):
    parts, heads, rows, dim = far_parts[0].shape
    seq_rows = 2 * (rows + PAD)
    n_head = len(grads)
    tokens = seq_rows // n_head
    margin = span + PAD
    edge = 2 * span + 3 * PAD
    mine = lambda h: (0, h, 0, 0)
    return call(
        functools.partial(attn_kernel, n_head, head0, span),
        16,
        0.01,
        grid=(heads,),
        in_specs=[pl.BlockSpec(memory_space=pltpu.SMEM)] * 2
        + [
            pl.BlockSpec((parts, 1, rows, dim), lambda h: (0, head0 + h, 0, 0)),
            pl.BlockSpec((parts, 1, rows, dim), mine),
            pl.BlockSpec((parts, 1, PAD, dim), mine),
            pl.BlockSpec((parts, 1, PAD, dim), mine),
            pl.BlockSpec((1, 2 * margin + PAD, dim), lambda h: (h, 0, 0)),
            pl.BlockSpec(taps.shape, lambda h: (0, 0, 0, 0)),
        ]
        + [pl.BlockSpec((tokens, dim), lambda h: (0, head0 + h))] * n_head,
        out_specs=[
            pl.BlockSpec((parts, 1, span + seq_rows, dim), mine),
            pl.BlockSpec((1, edge, dim), lambda h: (h, 0, 0)),
        ],
        out_shape=[
            jax.ShapeDtypeStruct((parts, heads, span + seq_rows, dim), F32),
            jax.ShapeDtypeStruct((heads, edge, dim), BF16),
        ],
        scratch_shapes=[
            pltpu.VMEM((parts, margin + PAD, dim), F32),
            pltpu.VMEM((parts, span + seq_rows, dim), BF16),
            pltpu.VMEM((seq_rows, dim), BF16),
        ],
        name="attention",
    )(window, offsets, near, *far_parts, halo, taps, *grads)


def finish_kernel(n_head, head0, span, totals, carry, taps, *refs):
    outs, rows = refs[:-1], refs[-1]
    tokens = outs[0].shape[2]
    seq_rows = tokens * n_head
    me = lax.axis_index("head")
    head = head0 + pl.program_id(0)
    inner = lax.axis_index("seq") < lax.axis_size("seq") - 1

    rows[0, :seq_rows] = totals[0, 0, span:]
    for p in (1, 2):
        edge = seq_rows - span
        back = carry[0, (p - 1) * span : p * span].astype(F32)
        rows[p, :edge] = totals[p, 0, span:seq_rows]
        rows[p, edge:seq_rows] = totals[p, 0, seq_rows:] + jnp.where(inner, back, 0.0)
    for p in range(3):
        at = 2 * span + p * PAD
        rows[p, seq_rows:] = jnp.where(inner, carry[0, at : at + PAD].astype(F32), 0.0)
    for j in range(n_head):
        start = pl.multiple_of(jnp.bitwise_xor(me, j) * tokens, tokens)

        def part(p, c, j=j, start=start):
            outs[j][p, 0] = spread(rows, taps, head, p, start, tokens).astype(BF16)
            return c

        lax.fori_loop(0, 3, part, 0)


def finish(totals, carry, taps, head0, n_head, span):
    parts, heads, rows, dim = totals.shape
    seq_rows = rows - span
    tokens = seq_rows // n_head
    return call(
        functools.partial(finish_kernel, n_head, head0, span),
        16,
        2 * heads,
        grid=(heads,),
        in_specs=[
            pl.BlockSpec((parts, 1, rows, dim), lambda h: (0, h, 0, 0)),
            pl.BlockSpec((1, carry.shape[1], dim), lambda h: (h, 0, 0)),
            pl.BlockSpec(taps.shape, lambda h: (0, 0, 0, 0)),
        ],
        out_specs=[pl.BlockSpec((parts, 1, tokens, dim), lambda h: (0, h, 0, 0))] * n_head,
        out_shape=[jax.ShapeDtypeStruct((parts, heads, tokens, dim), BF16)] * n_head,
        scratch_shapes=[pltpu.VMEM((parts, seq_rows + PAD, dim), F32)],
        name="finish",
    )(totals, carry, taps)


def partner(value, j):
    if j == 0:
        return value
    size = lax.axis_size("head")
    return lax.ppermute(value, "head", [(i, i ^ j) for i in range(size)])


def shifted(value, by):
    length = lax.axis_size("seq")
    pairs = [(i, (i + by) % length) for i in range(length)]
    return lax.ppermute(value, "seq", pairs)


def tail_kernel(n_head, head0, span, *refs):
    pieces, out, sems = refs[:n_head], refs[n_head], refs[n_head + 1]
    tokens = pieces[0].shape[2]
    heads = out.shape[0]
    margin = span + PAD
    me = lax.axis_index("head")
    moves = []
    for p, rows, at in ((1, margin, 0), (2, margin, margin), (0, PAD, 2 * margin)):
        source = n_head - 1
        while rows > 0:
            take = min(rows, tokens)
            rows -= take
            moves.append((p, source, take, at + rows))
            source -= 1

    def move(i, j):
        p, _, take, at = moves[i]
        first = head0 if j < n_head // 2 else 0
        return pltpu.make_async_copy(
            pieces[j].at[p, first : first + heads, tokens - take :],
            out.at[:, at : at + take],
            sems.at[i],
        )

    for i, (_, source, _, _) in enumerate(moves):
        for j in range(n_head):
            pl.when(me == source ^ j)(lambda i=i, j=j: move(i, j).start())
    for i in range(len(moves)):
        move(i, 0).wait()


def tail_of(near, far, head0, span):
    pieces = list(near) + list(far)
    _, heads, tokens, dim = far[0].shape
    margin = span + PAD
    count = 2 * -(-margin // tokens) + 1
    return call(
        functools.partial(tail_kernel, len(pieces), head0, span),
        8,
        0.5,
        in_specs=[pl.BlockSpec(memory_space=pl.ANY)] * len(pieces),
        out_specs=pl.BlockSpec(memory_space=pl.ANY),
        out_shape=jax.ShapeDtypeStruct((heads, 2 * margin + PAD, dim), BF16),
        scratch_shapes=[pltpu.SemaphoreType.DMA((count,))],
        name="tail",
    )(*pieces)


def tied(*values):
    return lax.optimization_barrier(values)


def per_device(qkv_pre, grad_out, out_values, out_scales, conv_kernel, window, offsets):
    n_head = lax.axis_size("head")
    tokens, _, heads, dim = qkv_pre.shape
    local = heads // n_head
    n_chunks = 2 if local % 2 == 0 else 1
    per_chunk = local // n_chunks
    half = n_head // 2
    span = tokens * n_head // 4

    g_near = [partner(grad_out, j) for j in range(half)]
    g_far = partner(grad_out, half)
    near, far = pack(qkv_pre, n_head, n_chunks)
    near = [partner(near[j], j) for j in range(half)]
    far = [[partner(far[c][j], half + j) for j in range(half)] for c in range(n_chunks)]
    near, values, g_near = tied(near, out_values, g_near)
    weight = dequantize(values, out_scales)
    grads = list(d_attn(g_near, weight))
    near, grads = tied(near, grads)
    mixed_near = conv_near(near, conv_kernel)
    g_far, mixed_near = tied(g_far, mixed_near)
    far[0], g_far, mixed_near = tied(far[0], g_far, mixed_near)
    g_rest = [partner(g_far, j) for j in range(1, half)]

    halos, parts = [], []
    for c in range(n_chunks):
        if c > 0:
            far[c], parts, grads = tied(far[c], parts, grads)
        tail = tail_of(near, far[c], c * per_chunk, span)
        far[c], tail = tied(far[c], tail)
        halos.append(shifted(tail, 1))
        parts.append(conv_far(near, far[c], conv_kernel, c * per_chunk))
        if c == 0:
            g_rest, parts[0] = tied(g_rest, parts[0])
            grads += list(d_attn([g_far] + g_rest, weight))

    held = []
    parts, grads, halos[0] = tied(parts, grads, halos[0])
    for c in range(n_chunks):
        totals, carry = attention(
            mixed_near, parts[c], halos[c], grads, conv_kernel, window, offsets, c * per_chunk, span
        )
        if c + 1 < n_chunks:
            halos[c + 1], totals, carry = tied(halos[c + 1], totals, carry)
        held.append((totals, shifted(carry, -1)))
    results = []
    held[0], last = tied(held[0], held[-1][0])
    for c in range(n_chunks):
        outs = finish(*held[c], conv_kernel, c * per_chunk, n_head, span)
        if c > 0:
            sent, outs = tied(results[c - 1][: half + 1], outs)
            results[c - 1][: half + 1] = sent
        if c + 1 < n_chunks:
            outs, totals = tied(outs, held[c + 1][0])
            held[c + 1] = (totals, held[c + 1][1])
        results.append([partner(outs[j], j) for j in range(n_head)])
    return unpack(results, n_head, n_chunks)


def solution(mesh):
    return jax.shard_map(
        per_device,
        mesh=mesh,
        in_specs=(
            P(("seq", "head"), None, None, None),
            P(("seq", "head"), None),
            P("head", None),
            P(),
            P(None, None, "head", None),
            P(),
            P(),
        ),
        out_specs=P(("seq", "head"), None, None, None),
        check_vma=False,
    )
```
